256 devices in a mesh: row: 16 (over y, z_lo), col: 16 (over x, z_hi, core).
Axes of the slice: x: 4, y: 4, z: 8 (z_hi: 2, z_lo: 4; z = z_hi * 4 + z_lo), core: 2. Of those that a mesh axis runs over, the one named last changes fastest.
Arguments:
- matrix: bfloat16 [8192, 8192], P('row', 'col'), may hold values from 0 to 0.0024414062, as said below
- in_mask: int32 [32, 32], P('row', 'col'), may hold values from 0 to 1, as said below
- out_mask: int32 [32, 32], P('row', 'col'), may hold values from 0 to 1, as said below
Outputs:
- flow: float32 [8192, 8192], P('row', 'col')
The draws below stay inside these ranges and needn't reach their ends.
Inputs may be any that keep to these rules, and one draw needn't show every extreme that they name: `matrix`: every diagonal entry is positive; all other entries are zero or positive. `in_mask`: tiles on the diagonal are 1. The block of tiles of one device holds at most 3 ones, and some device's block holds exactly 3. `out_mask`: tiles on the diagonal are 1.
All inputs are finite; a program needn't handle non-finite values.
Results may differ from the reference program's by a relative error of at most 0.0003.
Values may be sent and summed in bfloat16 or wider, within the bound.
A program may use at most 128 MiB of HBM per device.

```python
import jax
import jax.numpy as jnp
from jax import lax

TILE = 256
NT = 32
ROWS = 8192
N_ROW = 16
N_COL = 16


def draw_matrix(key, part):
    key = jax.random.fold_in(key, 11)
    key_keep = jax.random.fold_in(key, 1)
    key_value = jax.random.fold_in(key, 2)
    low = 0.05 / ROWS
    high = 20.0 / ROWS
    keep_bits = jax.random.randint(key_keep, (ROWS, ROWS), 0, 4)
    rows_index = jnp.arange(ROWS)[:, None]
    cols_index = jnp.arange(ROWS)[None, :]
    keep = (keep_bits < 2) | (rows_index == cols_index)
    values = jnp.exp(jax.random.uniform(key_value, (ROWS, ROWS), jnp.float32, jnp.log(low), jnp.log(high)))
    return jnp.where(keep, values, 0.0).astype(jnp.bfloat16)


def draw_in_mask(key, part):
    key = jax.random.fold_in(key, 23)
    block_rows = NT // N_ROW
    block_cols = NT // N_COL
    most = block_rows * block_cols * 3 // 4
    floor_count = min(block_rows, block_cols)
    row_level = jax.random.randint(jax.random.fold_in(key, 1), (N_ROW,), 1, most + 1)
    col_level = jax.random.randint(jax.random.fold_in(key, 2), (N_COL,), 1, most + 1)
    counts = jnp.clip(1 + row_level[:, None] * col_level[None, :] // most, floor_count, most)
    chosen_row = jax.random.randint(jax.random.fold_in(key, 3), (), 0, N_ROW)
    chosen_col = jax.random.randint(jax.random.fold_in(key, 4), (), 0, N_COL)
    forced = (jnp.arange(N_ROW)[:, None] == chosen_row) & (jnp.arange(N_COL)[None, :] == chosen_col)
    counts = jnp.where(forced, most, counts).astype(jnp.int32)
    flat_index = (jnp.arange(NT)[:, None] * NT + jnp.arange(NT)[None, :]).astype(jnp.int32)
    scores = jax.random.randint(jax.random.fold_in(key, 5), (NT, NT), 0, 4096) * (NT * NT) + flat_index
    diagonal = jnp.arange(NT)[:, None] == jnp.arange(NT)[None, :]
    scores = jnp.where(diagonal, flat_index - NT * NT, scores).astype(jnp.int32)
    blocks = scores.reshape(N_ROW, block_rows, N_COL, block_cols).transpose(0, 2, 1, 3).reshape(N_ROW, N_COL, block_rows * block_cols)
    ranks = jnp.argsort(jnp.argsort(blocks, axis=-1), axis=-1)
    keep = (ranks < counts[:, :, None]).astype(jnp.int32)
    return keep.reshape(N_ROW, N_COL, block_rows, block_cols).transpose(0, 2, 1, 3).reshape(NT, NT)


def draw_out_mask(key, part):
    key = jax.random.fold_in(key, 37)
    rolled = jax.random.randint(key, (NT, NT), 0, 2)
    diagonal = jnp.arange(NT)[:, None] == jnp.arange(NT)[None, :]
    return ((rolled == 1) | diagonal).astype(jnp.int32)


def setup_inputs(seed: int = 0) -> dict:
    streams_of = jax.random.split(jax.random.key(seed), 4)
    matrix = draw_matrix(jax.random.fold_in(streams_of[3], 71), 0)
    in_mask = draw_in_mask(jax.random.fold_in(streams_of[3], 71), 0)
    out_mask = draw_out_mask(jax.random.fold_in(streams_of[3], 71), 0)
    return {"matrix": matrix, "in_mask": in_mask, "out_mask": out_mask}


def expand_tiles(tile_flags):
    return jnp.repeat(jnp.repeat(tile_flags, TILE, axis=0), TILE, axis=1).astype(jnp.float32)


def reference(matrix, in_mask, out_mask):
    active = matrix.astype(jnp.float32) * expand_tiles(in_mask)
    product = jnp.dot(active, active, precision=lax.Precision.HIGHEST, preferred_element_type=jnp.float32)
    inflated = product * product * expand_tiles(out_mask)
    totals = jnp.sum(inflated, axis=0)
    return float(ROWS) * inflated / totals[None, :]
```

```python
import functools

import jax
import jax.numpy as jnp
from jax import lax
from jax.experimental import pallas as pl
from jax.experimental.pallas import tpu as pltpu
from jax.sharding import PartitionSpec as P

MESH = pl.DeviceIdType.MESH
T = 256
N = 2 * T
BODY = 3 * T
ROWS = BODY + 16
CUT = 400
HALF = ((0, CUT), (CUT, ROWS - CUT))
PAIRS = tuple((t, s) for t in range(4) for s in range(3) if s <= t)


def kernel(
    total_rows, m_ref, in_ref, om_ref, infl_ref, scale_ref,
    abuf, bbuf, ad, bd, acc, tot, part,
    ys, yr, zs, zr, xs, xr, cs, cr, ss, sr, ts, tr, osem,
):
    row = lax.axis_index("row")
    col = lax.axis_index("col")
    y, z = row // 4, row % 4
    x, h, core = col // 4, (col // 2) % 2, col % 2
    hi = z // 2
    yup, ydn = (y + 1) % 4, (y + 3) % 4
    xup, xdn = (x + 1) % 4, (x + 3) % 4
    zorder = (z, 1 - z + 4 * hi, 2 - hi, 3 - 3 * hi)
    horder = (h, 1 - h)

    def col_of(xx, hh, kk):
        return xx * 4 + hh * 2 + kk

    barrier = pltpu.get_barrier_semaphore()

    def greet(d, _):
        pl.semaphore_signal(barrier, inc=1, device_id=((row + d) % 16, col), device_id_type=MESH)
        return 0

    lax.fori_loop(1, 16, greet, 0)
    for c in (col_of(xup, h, core), col_of(xdn, h, core), col_of(x, 1 - h, core), col_of(x, h, 1 - core)):
        pl.semaphore_signal(barrier, inc=1, device_id=(row, c), device_id_type=MESH)

    flags = [in_ref[0, 0], in_ref[0, 1], in_ref[1, 0], in_ref[1, 1]]
    ranks = [0, flags[0], flags[0] + flags[1], flags[0] + flags[1] + flags[2]]
    here = {(t, s): jnp.logical_and(flags[t] == 1, ranks[t] == s) for t, s in PAIRS}
    mine_b = row
    mine_a = col
    for s in range(3):
        for r in range(0, T, 64):
            value = jnp.zeros((64, T), jnp.bfloat16)
            for t in range(s, 4):
                i, j = t // 2, t % 2
                tile = m_ref[i * T + r : i * T + r + 64, j * T : (j + 1) * T]
                value = lax.select(here[t, s], tile, value)
            bbuf[mine_b, pl.ds(s * T + r, 64), :] = value
            abuf[mine_a, pl.ds(s * T + r, 64), :] = value
    line = lax.broadcasted_iota(jnp.int32, (16, T), 0)
    weights = jnp.zeros((16, T), jnp.float32)
    for q, (t, s) in enumerate(PAIRS):
        weights = jnp.where(line == q, here[t, s].astype(jnp.float32), weights)
    weights = weights.astype(jnp.bfloat16)
    bbuf[mine_b, pl.ds(BODY, 16), :] = weights
    abuf[mine_a, pl.ds(BODY, 16), :] = weights

    pl.semaphore_wait(barrier, 19)

    def whole(buf, k, send, recv, device):
        return pltpu.make_async_remote_copy(
            src_ref=buf.at[k], dst_ref=buf.at[k], send_sem=send, recv_sem=recv,
            device_id=device, device_id_type=MESH,
        )

    def half(buf, k, p, send, recv, device):
        at = buf.at[k, pl.ds(*HALF[p]), :]
        return pltpu.make_async_remote_copy(
            src_ref=at, dst_ref=at, send_sem=send, recv_sem=recv,
            device_id=device, device_id_type=MESH,
        )

    def y_copy(i, way, piece):
        to = ((yup, ydn)[way] * 4 + z, col)
        if piece < 2:
            which, origin = (way, 1 - way)[piece], y
        else:
            which, origin = way, (ydn, yup)[way]
        return half(bbuf, origin * 4 + zorder[i], which, ys.at[i, way, piece], yr.at[i, way, piece], to)

    def y_arrival(i, way, piece):
        if piece < 2:
            which, origin = (way, 1 - way)[piece], (ydn, yup)[way]
        else:
            which, origin = way, (y + 2) % 4
        return half(bbuf, origin * 4 + zorder[i], which, ys.at[i, way, piece], yr.at[i, way, piece], ((yup, ydn)[way] * 4 + z, col))

    def x_copy(i, way, piece):
        to = (row, col_of((xup, xdn)[way], h, core))
        if piece < 2:
            which, origin = (way, 1 - way)[piece], x
        else:
            which, origin = way, (xdn, xup)[way]
        return half(abuf, col_of(origin, horder[i], core), which, xs.at[i, way, piece], xr.at[i, way, piece], to)

    def x_arrival(i, way, piece):
        if piece < 2:
            which, origin = (way, 1 - way)[piece], (xdn, xup)[way]
        else:
            which, origin = way, (x + 2) % 4
        return half(abuf, col_of(origin, horder[i], core), which, xs.at[i, way, piece], xr.at[i, way, piece], (row, col_of((xup, xdn)[way], h, core)))

    def s_copy(i, d):
        k = col_of((x + d) % 4, horder[i], core)
        return whole(abuf, k, ss.at[i, d], sr.at[i, d], (row, col_of(x, h, 1 - core)))

    def s_arrival(i, d):
        k = col_of((x + d) % 4, horder[i], 1 - core)
        return whole(abuf, k, ss.at[i, d], sr.at[i, d], (row, col_of(x, h, 1 - core)))

    cross = whole(abuf, mine_a, cs, cr, (row, col_of(x, 1 - h, core)))
    crossed = whole(abuf, col_of(x, 1 - h, core), cs, cr, (row, col_of(x, 1 - h, core)))

    z_up = whole(bbuf, row, zs.at[0], zr.at[z], (row + 1, col))
    z_down = whole(bbuf, row, zs.at[1], zr.at[z], (row - 1, col))
    has_up, has_down = z < 3, z > 0
    interior = jnp.logical_and(has_up, has_down)
    at_end = jnp.logical_not(interior)

    def z_forward(i):
        to = y * 4 + (3 - z if i == 1 else 3 * hi)
        k = y * 4 + zorder[i]
        return whole(bbuf, k, zs.at[1 + i], zr.at[zorder[i]], (to, col))

    def z_arrival(i):
        k = y * 4 + zorder[i]
        return whole(bbuf, k, zs.at[1 + i], zr.at[zorder[i]], (y * 4 + (z + 1) % 4, col))

    def y_send(i):
        for piece in range(2):
            for way in range(2):
                y_copy(i, way, piece).start()

    def y_turn(i):
        for way in range(2):
            y_arrival(i, way, 0).wait_recv()
            y_copy(i, way, 2).start()

    def x_send(i):
        for piece in range(2):
            for way in range(2):
                x_copy(i, way, piece).start()

    def x_turn(i):
        for way in range(2):
            x_arrival(i, way, 0).wait_recv()
            x_copy(i, way, 2).start()

    def z_turn(i):
        z_arrival(i).wait_recv()
        pl.when(interior)(lambda: z_forward(i).start())

    def x_near(i):
        for way in range(2):
            x_arrival(i, way, 1).wait_recv()
            s_copy(i, (3, 1)[way]).start()

    def x_far(i):
        for way in range(2):
            x_arrival(i, way, 2).wait_recv()
        s_copy(i, 2).start()

    def expand(buf, k, to):
        ext = buf[k, pl.ds(BODY, 16), :].astype(jnp.float32)
        w = {
            ts_: jnp.broadcast_to(ext[q : q + 1, :], (16, T)).astype(jnp.bfloat16)[None]
            for q, ts_ in enumerate(PAIRS)
        }
        for t in range(4):
            i, j = t // 2, t % 2
            value = None
            for s in range(min(t, 2) + 1):
                term = buf[k, pl.ds(s * T, T), :].reshape(16, 16, T) * w[t, s]
                value = term if value is None else value + term
            to[i * T : (i + 1) * T, j * T : (j + 1) * T] = value.reshape(T, T)

    def product(k):
        expand(abuf, k, ad)
        expand(bbuf, k, bd)
        acc[...] += jnp.dot(ad[...], bd[...], preferred_element_type=jnp.float32)

    def products(i, offsets):
        first, count = offsets
        lax.fori_loop(first, first + count, lambda d, _: (product(((y + d) % 4) * 4 + zorder[i]), 0)[1], 0)

    @pl.when(has_up)
    def _():
        z_up.start()

    @pl.when(has_down)
    def _():
        z_down.start()

    y_send(0)
    x_send(0)
    s_copy(0, 0).start()
    acc[...] = jnp.zeros_like(acc)
    y_turn(0)
    x_turn(0)
    z_turn(1)
    pl.when(interior)(lambda: z_turn(2))
    cross.start()
    y_send(1)
    x_near(0)
    x_far(0)
    y_turn(1)
    pl.when(interior)(lambda: z_turn(3))
    pl.when(at_end)(lambda: z_arrival(2).wait_recv())
    y_send(2)
    crossed.wait_recv()
    x_send(1)
    s_copy(1, 0).start()
    y_turn(2)
    pl.when(at_end)(lambda: z_arrival(3).wait_recv())
    y_send(3)
    x_turn(1)
    x_near(1)
    x_far(1)
    for i in range(2):
        for d in range(4):
            s_arrival(i, d).wait_recv()

    def y_rest(i):
        for way in range(2):
            y_arrival(i, way, 1).wait_recv()
            y_arrival(i, way, 2).wait_recv()

    y_rest(0)
    products(0, (0, 4))
    y_turn(3)
    y_rest(1)
    products(1, (0, 4))
    y_rest(2)
    products(2, (0, 4))
    products(3, (0, 1))
    for way in range(2):
        y_arrival(3, way, 1).wait_recv()
    products(3, (1, 1))
    products(3, (3, 1))
    for way in range(2):
        y_arrival(3, way, 2).wait_recv()
    products(3, (2, 1))

    sums = jnp.zeros((8, N), jnp.float32)
    pieces = [[None, None], [None, None]]
    for i in range(2):
        keep = [(om_ref[i, j] == 1).astype(jnp.float32) for j in range(2)]
        for r in range(i * T, (i + 1) * T, 32):
            for j in range(2):
                at = (slice(r, r + 32), slice(j * T, (j + 1) * T))
                p = acc[at]
                v = p * p * keep[j]
                acc[at] = v
                v = v.reshape(4, 8, T).sum(axis=0)
                pieces[i][j] = v if pieces[i][j] is None else pieces[i][j] + v
    sums = jnp.concatenate([pieces[0][j] + pieces[1][j] for j in range(2)], axis=1)
    sums = jnp.sum(sums, axis=0, keepdims=True)
    part[...] = sums
    tot[row] = sums

    def t_copy(d):
        return pltpu.make_async_remote_copy(
            src_ref=part, dst_ref=tot.at[row], send_sem=ts.at[d], recv_sem=tr.at[d],
            device_id=((row + d) % 16, col), device_id_type=MESH,
        )

    def t_arrival(d):
        return pltpu.make_async_remote_copy(
            src_ref=part, dst_ref=tot.at[(row + 16 - d) % 16], send_sem=ts.at[d], recv_sem=tr.at[d],
            device_id=((row + d) % 16, col), device_id_type=MESH,
        )

    lax.fori_loop(1, 16, lambda d, _: (t_copy(d).start(), 0)[1], 0)
    out = pltpu.make_async_copy(acc, infl_ref, osem)
    out.start()
    lax.fori_loop(1, 16, lambda d, _: (t_arrival(d).wait_recv(), 0)[1], 0)
    total = tot[0]
    for d in range(1, 16):
        total = total + tot[d]
    scale_ref[...] = 1.0 / total
    out.wait()

    lax.fori_loop(1, 16, lambda d, _: (t_copy(d).wait_send(), 0)[1], 0)
    for i in range(4):
        for way in range(2):
            for piece in range(3):
                y_copy(i, way, piece).wait_send()
    for i in range(2):
        for way in range(2):
            for piece in range(3):
                x_copy(i, way, piece).wait_send()
        for d in range(4):
            s_copy(i, d).wait_send()
    cross.wait_send()

    @pl.when(has_up)
    def _():
        z_up.wait_send()

    @pl.when(has_down)
    def _():
        z_down.wait_send()

    @pl.when(interior)
    def _():
        for i in range(1, 4):
            z_forward(i).wait_send()


def solution(mesh):
    def step(matrix, in_mask, out_mask):
        total_rows = float(N * mesh.shape["row"])
        dma = pltpu.SemaphoreType.DMA
        inflated, scale = pl.pallas_call(
            functools.partial(kernel, total_rows),
            out_shape=(
                jax.ShapeDtypeStruct((N, N), jnp.float32),
                jax.ShapeDtypeStruct((1, N), jnp.float32),
            ),
            in_specs=[
                pl.BlockSpec(memory_space=pltpu.VMEM),
                pl.BlockSpec(memory_space=pltpu.SMEM),
                pl.BlockSpec(memory_space=pltpu.SMEM),
            ],
            out_specs=(
                pl.BlockSpec(memory_space=pl.ANY),
                pl.BlockSpec(memory_space=pltpu.VMEM),
            ),
            scratch_shapes=[
                pltpu.VMEM((16, ROWS, T), jnp.bfloat16),
                pltpu.VMEM((16, ROWS, T), jnp.bfloat16),
                pltpu.VMEM((N, N), jnp.bfloat16),
                pltpu.VMEM((N, N), jnp.bfloat16),
                pltpu.VMEM((N, N), jnp.float32),
                pltpu.VMEM((16, 1, N), jnp.float32),
                pltpu.VMEM((1, N), jnp.float32),
                dma((4, 2, 3)), dma((4, 2, 3)),
                dma((5,)), dma((4,)),
                dma((2, 2, 3)), dma((2, 2, 3)),
                dma, dma,
                dma((2, 4)), dma((2, 4)),
                dma((16,)), dma((16,)),
                dma,
            ],
            compiler_params=pltpu.CompilerParams(
                collective_id=0, has_side_effects=True, vmem_limit_bytes=40 * 1024 * 1024
            ),
            name="gather_square",
        )(matrix, in_mask, out_mask)
        return (total_rows * inflated) * scale

    placed = (P("row", "col"), P("row", "col"), P("row", "col"))
    return jax.shard_map(
        step, mesh=mesh, in_specs=placed, out_specs=P("row", "col"), check_vma=False
    )
```

```python
import jax
import jax.numpy as jnp
from jax import lax
from jax.experimental import pallas as pl
from jax.experimental.pallas import tpu as pltpu
from jax.sharding import PartitionSpec as P

MESH = pl.DeviceIdType.MESH
T = 256
N = 2 * T
LANES = 128
SLOT = 2 * T
BODY = 3 * SLOT
ROWS = BODY + 16
CUT = 784
HALF = ((0, CUT), (CUT, ROWS - CUT))
XCUT = (HALF, ((0, 464), (464, 448), (912, 384), (1296, 256)))
PAIRS = tuple((t, s) for t in range(4) for s in range(3) if s <= t)


def kernel(
    m_hbm, masks_hbm, infl_ref, scale_ref,
    m_ref, masks, abuf, bbuf, ad, bd, acc, tot, part,
    ys, yr, zs, zr, xs, xr, fs, fr, cs, cr, ss, sr, ts, tr, osem, isem,
):
    row = lax.axis_index("row")
    col = lax.axis_index("col")
    y, z = row // 4, row % 4
    x, h, core = col // 4, (col // 2) % 2, col % 2
    hi = z // 2
    yup, ydn = (y + 1) % 4, (y + 3) % 4
    xup, xdn = (x + 1) % 4, (x + 3) % 4
    zorder = (z, 1 - z + 4 * hi, 2 - hi, 3 - 3 * hi)
    horder = (h, 1 - h)

    def col_of(xx, hh, kk):
        return xx * 4 + hh * 2 + kk

    loads = [
        pltpu.make_async_copy(src, dst, isem.at[n])
        for n, (src, dst) in enumerate(((masks_hbm, masks), (m_hbm, m_ref)))
    ]
    for load in loads:
        load.start()

    barrier = pltpu.get_barrier_semaphore()

    def greet(d, _):
        pl.semaphore_signal(barrier, inc=1, device_id=((row + d) % 16, col), device_id_type=MESH)
        return 0

    lax.fori_loop(1, 16, greet, 0)
    for c in (col_of(xup, h, core), col_of(xdn, h, core), col_of(x, 1 - h, core), col_of(x, h, 1 - core)):
        pl.semaphore_signal(barrier, inc=1, device_id=(row, c), device_id_type=MESH)

    for load in loads:
        load.wait()
    flags = [masks[0, 0], masks[0, 1], masks[1, 0], masks[1, 1]]
    ranks = [0, flags[0], flags[0] + flags[1], flags[0] + flags[1] + flags[2]]
    here = {(t, s): jnp.logical_and(flags[t] == 1, ranks[t] == s) for t, s in PAIRS}
    mine_b = row
    mine_a = col
    for s in range(3):
        for r in range(0, T, 64):
            value = jnp.zeros((64, T), jnp.bfloat16)
            for t in range(s, 4):
                i, j = t // 2, t % 2
                tile = m_ref[i * T + r : i * T + r + 64, j * T : (j + 1) * T]
                value = lax.select(here[t, s], tile, value)
            for e in range(2):
                at = pl.ds(s * SLOT + e * T + r, 64)
                bbuf[mine_b, at, :] = value[:, e * LANES : (e + 1) * LANES]
                abuf[mine_a, at, :] = value[:, e * LANES : (e + 1) * LANES]
    line = lax.broadcasted_iota(jnp.int32, (16, LANES), 0)
    weights = jnp.zeros((16, LANES), jnp.float32)
    for q, (t, s) in enumerate(PAIRS):
        weights = jnp.where(line == q, here[t, s].astype(jnp.float32), weights)
    weights = weights.astype(jnp.bfloat16)
    bbuf[mine_b, pl.ds(BODY, 16), :] = weights
    abuf[mine_a, pl.ds(BODY, 16), :] = weights

    pl.semaphore_wait(barrier, 19)

    def whole(buf, k, send, recv, device):
        return pltpu.make_async_remote_copy(
            src_ref=buf.at[k], dst_ref=buf.at[k], send_sem=send, recv_sem=recv,
            device_id=device, device_id_type=MESH,
        )

    def half(buf, k, p, send, recv, device):
        at = buf.at[k, pl.ds(*HALF[p]), :]
        return pltpu.make_async_remote_copy(
            src_ref=at, dst_ref=at, send_sem=send, recv_sem=recv,
            device_id=device, device_id_type=MESH,
        )

    def y_copy(i, way, piece):
        to = ((yup, ydn)[way] * 4 + z, col)
        if piece < 2:
            which, origin = (way, 1 - way)[piece], y
        else:
            which, origin = way, (ydn, yup)[way]
        return half(bbuf, origin * 4 + zorder[i], which, ys.at[i, way, piece], yr.at[i, way, piece], to)

    def y_arrival(i, way, piece):
        if piece < 2:
            which, origin = (way, 1 - way)[piece], (ydn, yup)[way]
        else:
            which, origin = way, (y + 2) % 4
        return half(bbuf, origin * 4 + zorder[i], which, ys.at[i, way, piece], yr.at[i, way, piece], ((yup, ydn)[way] * 4 + z, col))

    def x_piece(i, origin, q, send, recv, way):
        at = abuf.at[col_of(origin, horder[i], core), pl.ds(*XCUT[i][q]), :]
        return pltpu.make_async_remote_copy(
            src_ref=at, dst_ref=at, send_sem=send, recv_sem=recv,
            device_id=(row, col_of((xup, xdn)[way], h, core)), device_id_type=MESH,
        )

    def x_copy(i, way, q):
        return x_piece(i, x, q, xs.at[i, way, q], xr.at[i, way, q], way)

    def x_arrival(i, way, q):
        return x_piece(i, (xdn, xup)[way], q, xs.at[i, way, q], xr.at[i, way, q], way)

    def x_forward(i, q):
        return x_piece(i, (xdn, xup)[q % 2], q, fs.at[i, q], fr.at[i, q], q % 2)

    def x_forwarded(i, q):
        return x_piece(i, (x + 2) % 4, q, fs.at[i, q], fr.at[i, q], q % 2)

    def s_piece(i, d, q, kk):
        at = abuf.at[col_of((x + d) % 4, horder[i], kk), pl.ds(*XCUT[i][q]), :]
        return pltpu.make_async_remote_copy(
            src_ref=at, dst_ref=at, send_sem=ss.at[i, d, q], recv_sem=sr.at[i, d, q],
            device_id=(row, col_of(x, h, 1 - core)), device_id_type=MESH,
        )

    def s_copy(i, d, q):
        return s_piece(i, d, q, core)

    def s_arrival(i, d):
        for q in range(len(XCUT[i])):
            s_piece(i, d, q, 1 - core).wait_recv()

    def cross(q, k=None):
        at = abuf.at[mine_a if k is None else k, pl.ds(*XCUT[1][q]), :]
        return pltpu.make_async_remote_copy(
            src_ref=at, dst_ref=at, send_sem=cs.at[q], recv_sem=cr.at[q],
            device_id=(row, col_of(x, 1 - h, core)), device_id_type=MESH,
        )

    def crossed(q):
        return cross(q, col_of(x, 1 - h, core))

    z_up = whole(bbuf, row, zs.at[0], zr.at[z], (row + 1, col))
    z_down = whole(bbuf, row, zs.at[1], zr.at[z], (row - 1, col))
    has_up, has_down = z < 3, z > 0
    interior = jnp.logical_and(has_up, has_down)
    at_end = jnp.logical_not(interior)

    def z_forward(i):
        to = y * 4 + (3 - z if i == 1 else 3 * hi)
        k = y * 4 + zorder[i]
        return whole(bbuf, k, zs.at[1 + i], zr.at[zorder[i]], (to, col))

    def z_arrival(i):
        k = y * 4 + zorder[i]
        return whole(bbuf, k, zs.at[1 + i], zr.at[zorder[i]], (y * 4 + (z + 1) % 4, col))

    def y_send(i):
        for piece in range(2):
            for way in range(2):
                y_copy(i, way, piece).start()

    def y_turn(i):
        for way in range(2):
            y_arrival(i, way, 0).wait_recv()
            y_copy(i, way, 2).start()

    def x_send(i, q):
        for way in (q % 2, 1 - q % 2):
            x_copy(i, way, q).start()

    def x_cross(q):
        crossed(q).wait_recv()
        x_send(1, q)
        s_copy(1, 0, q).start()

    def x_turn(i, q):
        x_arrival(i, q % 2, q).wait_recv()
        x_forward(i, q).start()
        s_copy(i, (3, 1)[q % 2], q).start()

    def x_near(i, q):
        x_arrival(i, 1 - q % 2, q).wait_recv()
        s_copy(i, (1, 3)[q % 2], q).start()

    def x_far(i, q):
        x_forwarded(i, q).wait_recv()
        s_copy(i, 2, q).start()

    def z_turn(i):
        z_arrival(i).wait_recv()
        pl.when(interior)(lambda: z_forward(i).start())

    def s_rest(i):
        for d in range(4):
            s_arrival(i, d)

    def y_rest(i):
        for way in range(2):
            y_arrival(i, way, 1).wait_recv()
            y_arrival(i, way, 2).wait_recv()

    def expand(buf, k, to):
        ext = buf[k, pl.ds(BODY, 16), :].astype(jnp.float32)
        w = {
            at: jnp.broadcast_to(ext[q : q + 1, :], (16, LANES)).astype(jnp.bfloat16)[None]
            for q, at in enumerate(PAIRS)
        }
        for t in range(4):
            i, j = t // 2, t % 2
            for e in range(2):
                value = None
                for s in range(min(t, 2) + 1):
                    part_of = buf[k, pl.ds(s * SLOT + e * T, T), :]
                    term = part_of.reshape(16, 16, LANES) * w[t, s]
                    value = term if value is None else value + term
                left = j * T + e * LANES
                to[i * T : (i + 1) * T, left : left + LANES] = value.reshape(T, LANES)

    def product(k):
        expand(abuf, k, ad)
        expand(bbuf, k, bd)
        acc[...] += jnp.dot(ad[...], bd[...], preferred_element_type=jnp.float32)

    def products(i, first, count=4, stride=1):
        def one(n, _):
            product(((first + n * stride) % 4) * 4 + zorder[i])
            return 0

        lax.fori_loop(0, count, one, 0)

    near = hi == h
    far = hi != h

    def late(first, count):
        @pl.when(far)
        def _():
            products(0, x + first, count, 2)
            products(1, x + first, count, 2)

        pl.when(near)(lambda: products(2, x + first, count, 2))

    @pl.when(has_up)
    def _():
        z_up.start()

    @pl.when(has_down)
    def _():
        z_down.start()

    y_send(0)
    for q in range(2):
        x_send(0, q)
        s_copy(0, 0, q).start()
    cross(0).start()
    acc[...] = jnp.zeros_like(acc)
    y_turn(0)
    x_turn(0, 0)
    x_turn(0, 1)
    z_turn(1)
    pl.when(interior)(lambda: z_turn(2))
    y_send(1)
    cross(1).start()
    for q in range(2):
        x_near(0, q)
    for q in range(2):
        x_far(0, q)
    s_rest(0)
    y_rest(0)
    y_turn(1)
    pl.when(near)(lambda: products(0, y))
    pl.when(interior)(lambda: z_turn(3))
    pl.when(at_end)(lambda: z_arrival(2).wait_recv())
    y_send(2)
    cross(2).start()
    cross(3).start()
    x_cross(0)
    y_rest(1)
    pl.when(near)(lambda: products(1, y))
    x_turn(1, 0)
    x_near(1, 0)
    y_turn(2)
    pl.when(interior)(lambda: y_send(3))
    x_cross(1)
    x_far(1, 0)
    x_turn(1, 1)
    x_near(1, 1)

    @pl.when(at_end)
    def _():
        z_arrival(3).wait_recv()
        y_send(3)

    y_rest(2)

    @pl.when(far)
    def _():
        products(2, y)
        products(3, y, 1)

    x_cross(2)
    x_far(1, 1)
    y_turn(3)
    x_cross(3)
    x_turn(1, 2)
    x_turn(1, 3)
    x_near(1, 2)
    x_near(1, 3)
    s_arrival(1, 0)
    late(0, 1)
    x_far(1, 2)
    x_far(1, 3)
    s_arrival(1, 1)
    s_arrival(1, 3)
    late(1, 2)
    for way in range(2):
        y_arrival(3, way, 1).wait_recv()
    pl.when(jnp.logical_and(near, y != (x + 2) % 4))(lambda: products(3, y, 1))
    for d in (1, 3):
        pl.when(jnp.logical_or(far, (y + d) % 4 != (x + 2) % 4))(lambda d=d: products(3, y + d, 1))
    for way in range(2):
        y_arrival(3, way, 2).wait_recv()
    pl.when(jnp.logical_or(far, y != x))(lambda: products(3, y + 2, 1))
    s_arrival(1, 2)

    @pl.when(far)
    def _():
        products(0, x + 2, 1)
        products(1, x + 2, 1)

    @pl.when(near)
    def _():
        products(2, x + 2, 1)
        products(3, x + 2, 1)

    sums = jnp.zeros((8, N), jnp.float32)
    pieces = [[None, None], [None, None]]
    for i in range(2):
        keep = [(masks[2 + i, j] == 1).astype(jnp.float32) for j in range(2)]
        for r in range(i * T, (i + 1) * T, 32):
            for j in range(2):
                at = (slice(r, r + 32), slice(j * T, (j + 1) * T))
                p = acc[at]
                v = p * p * keep[j]
                acc[at] = v
                v = v.reshape(4, 8, T).sum(axis=0)
                pieces[i][j] = v if pieces[i][j] is None else pieces[i][j] + v
    sums = jnp.concatenate([pieces[0][j] + pieces[1][j] for j in range(2)], axis=1)
    sums = jnp.sum(sums, axis=0, keepdims=True)
    part[...] = sums
    tot[row] = sums

    def t_copy(d, i):
        to = (y + d) % 4 * 4 + zorder[i]
        return pltpu.make_async_remote_copy(
            src_ref=part, dst_ref=tot.at[row], send_sem=ts.at[d, i], recv_sem=tr.at[row],
            device_id=(to, col), device_id_type=MESH,
        )

    def t_arrival(d):
        k = (row + d) % 16
        return pltpu.make_async_remote_copy(
            src_ref=part, dst_ref=tot.at[k], send_sem=ts.at[0, 0], recv_sem=tr.at[k],
            device_id=(k, col), device_id_type=MESH,
        )

    peers = [(d, i) for d in (2, 1, 3, 0) for i in (3, 2, 1, 0) if d or i]
    peers.sort(key=lambda at: -(min(at[0], 2) % 3 - (at[0] == 3) + at[1]))
    for d, i in peers:
        t_copy(d, i).start()
    out = pltpu.make_async_copy(acc, infl_ref, osem)
    out.start()
    lax.fori_loop(1, 16, lambda d, _: (t_arrival(d).wait_recv(), 0)[1], 0)
    total = tot[0]
    for d in range(1, 16):
        total = total + tot[d]
    scale_ref[...] = 1.0 / total
    out.wait()

    for d, i in peers:
        t_copy(d, i).wait_send()
    for i in range(4):
        for way in range(2):
            for piece in range(3):
                y_copy(i, way, piece).wait_send()
    for i in range(2):
        for q in range(len(XCUT[i])):
            for way in range(2):
                x_copy(i, way, q).wait_send()
            x_forward(i, q).wait_send()
            for d in range(4):
                s_copy(i, d, q).wait_send()
    for q in range(4):
        cross(q).wait_send()

    @pl.when(has_up)
    def _():
        z_up.wait_send()

    @pl.when(has_down)
    def _():
        z_down.wait_send()

    @pl.when(interior)
    def _():
        for i in range(1, 4):
            z_forward(i).wait_send()


def solution(mesh):
    def step(matrix, in_mask, out_mask):
        total_rows = float(N * mesh.shape["row"])
        dma = pltpu.SemaphoreType.DMA
        inflated, scale = pl.pallas_call(
            kernel,
            out_shape=(
                jax.ShapeDtypeStruct((N, N), jnp.float32),
                jax.ShapeDtypeStruct((1, N), jnp.float32),
            ),
            in_specs=[
                pl.BlockSpec(memory_space=pltpu.HBM),
                pl.BlockSpec(memory_space=pltpu.HBM),
            ],
            out_specs=(
                pl.BlockSpec(memory_space=pl.ANY),
                pl.BlockSpec(memory_space=pltpu.VMEM),
            ),
            scratch_shapes=[
                pltpu.VMEM((N, N), jnp.bfloat16),
                pltpu.SMEM((4, 2), jnp.int32),
                pltpu.VMEM((16, ROWS, LANES), jnp.bfloat16),
                pltpu.VMEM((16, ROWS, LANES), jnp.bfloat16),
                pltpu.VMEM((N, N), jnp.bfloat16),
                pltpu.VMEM((N, N), jnp.bfloat16),
                pltpu.VMEM((N, N), jnp.float32),
                pltpu.VMEM((16, 1, N), jnp.float32),
                pltpu.VMEM((1, N), jnp.float32),
                dma((4, 2, 3)), dma((4, 2, 3)),
                dma((5,)), dma((4,)),
                dma((2, 2, 4)), dma((2, 2, 4)),
                dma((2, 4)), dma((2, 4)),
                dma((4,)), dma((4,)),
                dma((2, 4, 4)), dma((2, 4, 4)),
                dma((4, 4)), dma((16,)),
                dma, dma((3,)),
            ],
            compiler_params=pltpu.CompilerParams(
                collective_id=0, has_side_effects=True, vmem_limit_bytes=40 * 1024 * 1024
            ),
            name="gather_square",
        )(matrix, jnp.concatenate([in_mask, out_mask]))
        return (total_rows * inflated) * scale

    placed = (P("row", "col"), P("row", "col"), P("row", "col"))
    return jax.shard_map(
        step, mesh=mesh, in_specs=placed, out_specs=P("row", "col"), check_vma=False
    )
```

```python
import jax
import jax.numpy as jnp
from jax import lax
from jax.experimental import pallas as pl
from jax.experimental.pallas import tpu as pltpu
from jax.sharding import PartitionSpec as P

MESH = pl.DeviceIdType.MESH
T = 256
N = 2 * T
LANES = 128
SLOT = 2 * T
BODY = 3 * SLOT
ROWS = BODY + 16
CUT = 784
HALF = ((0, CUT), (CUT, ROWS - CUT))
XCUT = (HALF, ((0, 464), (464, 448), (912, 384), (1296, 256)))
PAIRS = tuple((t, s) for t in range(4) for s in range(3) if s <= t)


def kernel(
    m_hbm, masks_hbm, infl_ref, scale_ref,
    m_ref, masks, abuf, bbuf, ad, bd, acc, tot, part,
    ys, yr, zs, zr, xs, xr, fs, fr, cs, cr, ss, sr, ts, tr, osem, isem,
):
    row = lax.axis_index("row")
    col = lax.axis_index("col")
    y, z = row // 4, row % 4
    x, h, core = col // 4, (col // 2) % 2, col % 2
    hi = z // 2
    yup, ydn = (y + 1) % 4, (y + 3) % 4
    xup, xdn = (x + 1) % 4, (x + 3) % 4
    zorder = (z, 1 - z + 4 * hi, 2 - hi, 3 - 3 * hi)
    horder = (h, 1 - h)

    def col_of(xx, hh, kk):
        return xx * 4 + hh * 2 + kk

    loads = [
        pltpu.make_async_copy(src, dst, isem.at[n])
        for n, (src, dst) in enumerate(((masks_hbm, masks), (m_hbm, m_ref)))
    ]
    for load in loads:
        load.start()

    barrier = pltpu.get_barrier_semaphore()

    def greet(d, _):
        pl.semaphore_signal(barrier, inc=1, device_id=((row + d) % 16, col), device_id_type=MESH)
        return 0

    lax.fori_loop(1, 16, greet, 0)
    for c in (col_of(xup, h, core), col_of(xdn, h, core), col_of(x, 1 - h, core), col_of(x, h, 1 - core)):
        pl.semaphore_signal(barrier, inc=1, device_id=(row, c), device_id_type=MESH)

    for load in loads:
        load.wait()
    flags = [masks[0, 0], masks[0, 1], masks[1, 0], masks[1, 1]]
    ranks = [0, flags[0], flags[0] + flags[1], flags[0] + flags[1] + flags[2]]
    here = {(t, s): jnp.logical_and(flags[t] == 1, ranks[t] == s) for t, s in PAIRS}
    mine_b = row
    mine_a = col
    for s in range(3):
        for r in range(0, T, 64):
            value = jnp.zeros((64, T), jnp.bfloat16)
            for t in range(s, 4):
                i, j = t // 2, t % 2
                tile = m_ref[i * T + r : i * T + r + 64, j * T : (j + 1) * T]
                value = lax.select(here[t, s], tile, value)
            for e in range(2):
                at = pl.ds(s * SLOT + e * T + r, 64)
                bbuf[mine_b, at, :] = value[:, e * LANES : (e + 1) * LANES]
                abuf[mine_a, at, :] = value[:, e * LANES : (e + 1) * LANES]
    line = lax.broadcasted_iota(jnp.int32, (16, LANES), 0)
    weights = jnp.zeros((16, LANES), jnp.float32)
    for q, (t, s) in enumerate(PAIRS):
        weights = jnp.where(line == q, here[t, s].astype(jnp.float32), weights)
    weights = weights.astype(jnp.bfloat16)
    bbuf[mine_b, pl.ds(BODY, 16), :] = weights
    abuf[mine_a, pl.ds(BODY, 16), :] = weights

    pl.semaphore_wait(barrier, 19)

    def whole(buf, k, send, recv, device):
        return pltpu.make_async_remote_copy(
            src_ref=buf.at[k], dst_ref=buf.at[k], send_sem=send, recv_sem=recv,
            device_id=device, device_id_type=MESH,
        )

    def half(buf, k, p, send, recv, device):
        at = buf.at[k, pl.ds(*HALF[p]), :]
        return pltpu.make_async_remote_copy(
            src_ref=at, dst_ref=at, send_sem=send, recv_sem=recv,
            device_id=device, device_id_type=MESH,
        )

    def y_copy(i, way, piece):
        to = ((yup, ydn)[way] * 4 + z, col)
        if piece < 2:
            which, origin = (way, 1 - way)[piece], y
        else:
            which, origin = way, (ydn, yup)[way]
        return half(bbuf, origin * 4 + zorder[i], which, ys.at[i, way, piece], yr.at[i, way, piece], to)

    def y_arrival(i, way, piece):
        if piece < 2:
            which, origin = (way, 1 - way)[piece], (ydn, yup)[way]
        else:
            which, origin = way, (y + 2) % 4
        return half(bbuf, origin * 4 + zorder[i], which, ys.at[i, way, piece], yr.at[i, way, piece], ((yup, ydn)[way] * 4 + z, col))

    def x_piece(i, origin, q, send, recv, way):
        at = abuf.at[col_of(origin, horder[i], core), pl.ds(*XCUT[i][q]), :]
        return pltpu.make_async_remote_copy(
            src_ref=at, dst_ref=at, send_sem=send, recv_sem=recv,
            device_id=(row, col_of((xup, xdn)[way], h, core)), device_id_type=MESH,
        )

    def x_copy(i, way, q):
        return x_piece(i, x, q, xs.at[i, way, q], xr.at[i, way, q], way)

    def x_arrival(i, way, q):
        return x_piece(i, (xdn, xup)[way], q, xs.at[i, way, q], xr.at[i, way, q], way)

    def x_forward(i, q):
        return x_piece(i, (xdn, xup)[q % 2], q, fs.at[i, q], fr.at[i, q], q % 2)

    def x_forwarded(i, q):
        return x_piece(i, (x + 2) % 4, q, fs.at[i, q], fr.at[i, q], q % 2)

    def s_piece(i, d, q, kk):
        at = abuf.at[col_of((x + d) % 4, horder[i], kk), pl.ds(*XCUT[i][q]), :]
        return pltpu.make_async_remote_copy(
            src_ref=at, dst_ref=at, send_sem=ss.at[i, d, q], recv_sem=sr.at[i, d, q],
            device_id=(row, col_of(x, h, 1 - core)), device_id_type=MESH,
        )

    def s_copy(i, d, q):
        return s_piece(i, d, q, core)

    def s_arrival(i, d):
        for q in range(len(XCUT[i])):
            s_piece(i, d, q, 1 - core).wait_recv()

    def cross(q, k=None):
        at = abuf.at[mine_a if k is None else k, pl.ds(*XCUT[1][q]), :]
        return pltpu.make_async_remote_copy(
            src_ref=at, dst_ref=at, send_sem=cs.at[q], recv_sem=cr.at[q],
            device_id=(row, col_of(x, 1 - h, core)), device_id_type=MESH,
        )

    def crossed(q):
        return cross(q, col_of(x, 1 - h, core))

    z_up = whole(bbuf, row, zs.at[0], zr.at[z], (row + 1, col))
    z_down = whole(bbuf, row, zs.at[1], zr.at[z], (row - 1, col))
    has_up, has_down = z < 3, z > 0
    interior = jnp.logical_and(has_up, has_down)
    at_end = jnp.logical_not(interior)

    def z_forward(i):
        to = y * 4 + (3 - z if i == 1 else 3 * hi)
        k = y * 4 + zorder[i]
        return whole(bbuf, k, zs.at[1 + i], zr.at[zorder[i]], (to, col))

    def z_arrival(i):
        k = y * 4 + zorder[i]
        return whole(bbuf, k, zs.at[1 + i], zr.at[zorder[i]], (y * 4 + (z + 1) % 4, col))

    def y_send(i):
        for piece in range(2):
            for way in range(2):
                y_copy(i, way, piece).start()

    def y_turn(i):
        for way in range(2):
            y_arrival(i, way, 0).wait_recv()
            y_copy(i, way, 2).start()

    def x_send(i, q):
        for way in (q % 2, 1 - q % 2):
            x_copy(i, way, q).start()

    def x_cross(q):
        crossed(q).wait_recv()
        x_send(1, q)
        s_copy(1, 0, q).start()

    def x_turn(i, q):
        x_arrival(i, q % 2, q).wait_recv()
        x_forward(i, q).start()
        s_copy(i, (3, 1)[q % 2], q).start()

    def x_near(i, q):
        x_arrival(i, 1 - q % 2, q).wait_recv()
        s_copy(i, (1, 3)[q % 2], q).start()

    def x_far(i, q):
        x_forwarded(i, q).wait_recv()
        s_copy(i, 2, q).start()

    def z_turn(i):
        z_arrival(i).wait_recv()
        pl.when(interior)(lambda: z_forward(i).start())

    def s_rest(i):
        for d in range(4):
            s_arrival(i, d)

    def y_rest(i):
        for way in range(2):
            y_arrival(i, way, 1).wait_recv()
            y_arrival(i, way, 2).wait_recv()

    def expand(buf, k, to, r0, c0):
        ext = buf[k, pl.ds(BODY, 16), :].astype(jnp.float32)
        w = {
            at: jnp.broadcast_to(ext[q : q + 1, :], (16, LANES)).astype(jnp.bfloat16)[None]
            for q, at in enumerate(PAIRS)
        }
        for t in range(4):
            i, j = t // 2, t % 2
            for e in range(2):
                value = None
                for s in range(min(t, 2) + 1):
                    part_of = buf[k, pl.ds(s * SLOT + e * T, T), :]
                    term = part_of.reshape(16, 16, LANES) * w[t, s]
                    value = term if value is None else value + term
                left = j * T + e * LANES
                to[pl.ds(r0 + i * T, T), pl.ds(c0 + left, LANES)] = value.reshape(T, LANES)

    def open_a(i, first, count=4, stride=1):
        def one(n, _):
            k = (first + n // 2 * stride) % 4 * 4 + 2 * horder[i] + n % 2
            expand(abuf, k, ad, 0, pl.multiple_of(k * N, N))
            return 0

        lax.fori_loop(0, 2 * count, one, 0)

    def open_b(i, first, count=4, stride=1):
        def one(n, _):
            k = (first + n * stride) % 4 * 4 + zorder[i]
            expand(bbuf, k, bd, pl.multiple_of(k * N, N), 0)
            return 0

        lax.fori_loop(0, count, one, 0)

    def multiply(k, blocks):
        at = pl.ds(pl.multiple_of(k * N, N), blocks * N)
        acc[...] += jnp.dot(ad[:, at], bd[at, :], preferred_element_type=jnp.float32)

    def products(i, first, count=4, stride=1):
        def one(n, _):
            multiply((first + n * stride) % 4 * 4 + zorder[i], 1)
            return 0

        lax.fori_loop(0, count, one, 0)

    def doubles(hh, first, count=4, stride=1):
        def one(n, _):
            multiply((first + n * stride) % 4 * 4 + 2 * hh, 2)
            return 0

        lax.fori_loop(0, count, one, 0)

    near = hi == h
    far = hi != h

    def late(first, count):
        open_a(1, x + first, count, 2)
        pl.when(far)(lambda: doubles(hi, x + first, count, 2))
        pl.when(near)(lambda: products(2, x + first, count, 2))

    @pl.when(has_up)
    def _():
        z_up.start()

    @pl.when(has_down)
    def _():
        z_down.start()

    y_send(0)
    for q in range(2):
        x_send(0, q)
        s_copy(0, 0, q).start()
    cross(0).start()
    acc[...] = jnp.zeros_like(acc)
    y_turn(0)
    x_turn(0, 0)
    x_turn(0, 1)
    z_turn(1)
    pl.when(interior)(lambda: z_turn(2))
    y_send(1)
    for q in range(2):
        x_near(0, q)
    for q in range(2):
        x_far(0, q)
    s_rest(0)
    y_rest(0)
    y_turn(1)
    cross(1).start()
    open_a(0, x)
    open_b(0, y)
    pl.when(interior)(lambda: z_turn(3))
    pl.when(at_end)(lambda: z_arrival(2).wait_recv())
    y_send(2)
    cross(2).start()
    cross(3).start()
    x_cross(0)
    y_rest(1)
    open_b(1, y)
    pl.when(near)(lambda: doubles(h, y))
    x_turn(1, 0)
    x_near(1, 0)
    y_turn(2)
    pl.when(interior)(lambda: y_send(3))
    x_cross(1)
    x_far(1, 0)
    x_turn(1, 1)
    x_near(1, 1)

    @pl.when(at_end)
    def _():
        z_arrival(3).wait_recv()
        y_send(3)

    y_rest(2)

    open_b(2, y)
    open_b(3, y, 1)

    @pl.when(far)
    def _():
        products(2, y)
        products(3, y, 1)

    x_cross(2)
    x_far(1, 1)
    y_turn(3)
    x_cross(3)
    x_turn(1, 2)
    x_turn(1, 3)
    x_near(1, 2)
    x_near(1, 3)
    s_arrival(1, 0)
    late(0, 1)
    x_far(1, 2)
    x_far(1, 3)
    for way in range(2):
        y_arrival(3, way, 1).wait_recv()
    open_b(3, y + 1, 2, 2)
    pl.when(far)(lambda: products(3, y + 1, 2, 2))
    s_arrival(1, 1)
    s_arrival(1, 3)
    late(1, 2)
    for d in (0, 1, 3):
        pl.when(jnp.logical_and(near, (y + d) % 4 != (x + 2) % 4))(lambda d=d: products(3, y + d, 1))
    for way in range(2):
        y_arrival(3, way, 2).wait_recv()
    open_b(3, y + 2, 1)
    pl.when(jnp.logical_or(far, y != x))(lambda: products(3, y + 2, 1))
    s_arrival(1, 2)
    open_a(1, x + 2, 1)
    doubles(1 - h, x + 2, 1)

    sums = jnp.zeros((8, N), jnp.float32)
    pieces = [[None, None], [None, None]]
    for i in range(2):
        keep = [(masks[2 + i, j] == 1).astype(jnp.float32) for j in range(2)]
        for r in range(i * T, (i + 1) * T, 32):
            for j in range(2):
                at = (slice(r, r + 32), slice(j * T, (j + 1) * T))
                p = acc[at]
                v = p * p * keep[j]
                acc[at] = v
                v = v.reshape(4, 8, T).sum(axis=0)
                pieces[i][j] = v if pieces[i][j] is None else pieces[i][j] + v
    sums = jnp.concatenate([pieces[0][j] + pieces[1][j] for j in range(2)], axis=1)
    sums = jnp.sum(sums, axis=0, keepdims=True)
    part[...] = sums
    tot[row] = sums

    def t_copy(d, i):
        to = (y + d) % 4 * 4 + zorder[i]
        return pltpu.make_async_remote_copy(
            src_ref=part, dst_ref=tot.at[row], send_sem=ts.at[d, i], recv_sem=tr.at[row],
            device_id=(to, col), device_id_type=MESH,
        )

    def t_arrival(d):
        k = (row + d) % 16
        return pltpu.make_async_remote_copy(
            src_ref=part, dst_ref=tot.at[k], send_sem=ts.at[0, 0], recv_sem=tr.at[k],
            device_id=(k, col), device_id_type=MESH,
        )

    peers = [(d, i) for d in (2, 1, 3, 0) for i in (3, 2, 1, 0) if d or i]
    peers.sort(key=lambda at: -(min(at[0], 2) % 3 - (at[0] == 3) + at[1]))
    for d, i in peers:
        t_copy(d, i).start()
    out = pltpu.make_async_copy(acc, infl_ref, osem)
    out.start()
    lax.fori_loop(1, 16, lambda d, _: (t_arrival(d).wait_recv(), 0)[1], 0)
    total = tot[0]
    for d in range(1, 16):
        total = total + tot[d]
    scale_ref[...] = 1.0 / total
    out.wait()

    for d, i in peers:
        t_copy(d, i).wait_send()
    for i in range(4):
        for way in range(2):
            for piece in range(3):
                y_copy(i, way, piece).wait_send()
    for i in range(2):
        for q in range(len(XCUT[i])):
            for way in range(2):
                x_copy(i, way, q).wait_send()
            x_forward(i, q).wait_send()
            for d in range(4):
                s_copy(i, d, q).wait_send()
    for q in range(4):
        cross(q).wait_send()

    @pl.when(has_up)
    def _():
        z_up.wait_send()

    @pl.when(has_down)
    def _():
        z_down.wait_send()

    @pl.when(interior)
    def _():
        for i in range(1, 4):
            z_forward(i).wait_send()


def solution(mesh):
    def step(matrix, in_mask, out_mask):
        total_rows = float(N * mesh.shape["row"])
        dma = pltpu.SemaphoreType.DMA
        inflated, scale = pl.pallas_call(
            kernel,
            out_shape=(
                jax.ShapeDtypeStruct((N, N), jnp.float32),
                jax.ShapeDtypeStruct((1, N), jnp.float32),
            ),
            in_specs=[
                pl.BlockSpec(memory_space=pltpu.HBM),
                pl.BlockSpec(memory_space=pltpu.HBM),
            ],
            out_specs=(
                pl.BlockSpec(memory_space=pl.ANY),
                pl.BlockSpec(memory_space=pltpu.VMEM),
            ),
            scratch_shapes=[
                pltpu.VMEM((N, N), jnp.bfloat16),
                pltpu.SMEM((4, 2), jnp.int32),
                pltpu.VMEM((16, ROWS, LANES), jnp.bfloat16),
                pltpu.VMEM((16, ROWS, LANES), jnp.bfloat16),
                pltpu.VMEM((N, 16 * N), jnp.bfloat16),
                pltpu.VMEM((16 * N, N), jnp.bfloat16),
                pltpu.VMEM((N, N), jnp.float32),
                pltpu.VMEM((16, 1, N), jnp.float32),
                pltpu.VMEM((1, N), jnp.float32),
                dma((4, 2, 3)), dma((4, 2, 3)),
                dma((5,)), dma((4,)),
                dma((2, 2, 4)), dma((2, 2, 4)),
                dma((2, 4)), dma((2, 4)),
                dma((4,)), dma((4,)),
                dma((2, 4, 4)), dma((2, 4, 4)),
                dma((4, 4)), dma((16,)),
                dma, dma((3,)),
            ],
            compiler_params=pltpu.CompilerParams(
                collective_id=0, has_side_effects=True, vmem_limit_bytes=40 * 1024 * 1024
            ),
            name="gather_square",
        )(matrix, jnp.concatenate([in_mask, out_mask]))
        return (total_rows * inflated) * scale

    placed = (P("row", "col"), P("row", "col"), P("row", "col"))
    return jax.shard_map(
        step, mesh=mesh, in_specs=placed, out_specs=P("row", "col"), check_vma=False
    )
```

```python
import jax
import jax.numpy as jnp
from jax import lax
from jax.experimental import pallas as pl
from jax.experimental.pallas import tpu as pltpu
from jax.sharding import PartitionSpec as P

MESH = pl.DeviceIdType.MESH
T = 256
N = 2 * T
LANES = 128
SLOT = 2 * T
BODY = 3 * SLOT
ROWS = BODY + 16
CUT = 784
HALF = ((0, CUT), (CUT, ROWS - CUT))
XCUT = (HALF, ((0, 464), (464, 448), (912, 384), (1296, 256)))
PAIRS = tuple((t, s) for t in range(4) for s in range(3) if s <= t)


def kernel(
    m_hbm, masks_hbm, infl_ref, scale_ref,
    m_ref, masks, abuf, bbuf, ad, bd, acc, tot, part,
    ys, yr, zs, zr, xs, xr, fs, fr, cs, cr, ss, sr, ts, tr, osem, isem,
):
    row = lax.axis_index("row")
    col = lax.axis_index("col")
    y, z = row // 4, row % 4
    x, h, core = col // 4, (col // 2) % 2, col % 2
    hi = z // 2
    yup, ydn = (y + 1) % 4, (y + 3) % 4
    xup, xdn = (x + 1) % 4, (x + 3) % 4
    zorder = (z, 1 - z + 4 * hi, 2 - hi, 3 - 3 * hi)
    horder = (h, 1 - h)

    def col_of(xx, hh, kk):
        return xx * 4 + hh * 2 + kk

    loads = [
        pltpu.make_async_copy(src, dst, isem.at[n])
        for n, (src, dst) in enumerate(((masks_hbm, masks), (m_hbm, m_ref)))
    ]
    for load in loads:
        load.start()

    barrier = pltpu.get_barrier_semaphore()

    def greet(d, _):
        pl.semaphore_signal(barrier, inc=1, device_id=((row + d) % 16, col), device_id_type=MESH)
        return 0

    lax.fori_loop(1, 16, greet, 0)
    for c in (col_of(xup, h, core), col_of(xdn, h, core), col_of(x, 1 - h, core), col_of(x, h, 1 - core)):
        pl.semaphore_signal(barrier, inc=1, device_id=(row, c), device_id_type=MESH)

    for load in loads:
        load.wait()
    flags = [masks[0, 0], masks[0, 1], masks[1, 0], masks[1, 1]]
    ranks = [0, flags[0], flags[0] + flags[1], flags[0] + flags[1] + flags[2]]
    here = {(t, s): jnp.logical_and(flags[t] == 1, ranks[t] == s) for t, s in PAIRS}
    mine_b = row
    mine_a = col
    for s in range(3):
        for r in range(0, T, 64):
            value = jnp.zeros((64, T), jnp.bfloat16)
            for t in range(s, 4):
                i, j = t // 2, t % 2
                tile = m_ref[i * T + r : i * T + r + 64, j * T : (j + 1) * T]
                value = lax.select(here[t, s], tile, value)
            for e in range(2):
                at = pl.ds(s * SLOT + e * T + r, 64)
                bbuf[mine_b, at, :] = value[:, e * LANES : (e + 1) * LANES]
                abuf[mine_a, at, :] = value[:, e * LANES : (e + 1) * LANES]
    line = lax.broadcasted_iota(jnp.int32, (16, LANES), 0)
    weights = jnp.zeros((16, LANES), jnp.float32)
    for q, (t, s) in enumerate(PAIRS):
        weights = jnp.where(line == q, here[t, s].astype(jnp.float32), weights)
    weights = weights.astype(jnp.bfloat16)
    bbuf[mine_b, pl.ds(BODY, 16), :] = weights
    abuf[mine_a, pl.ds(BODY, 16), :] = weights

    pl.semaphore_wait(barrier, 19)

    def whole(buf, k, send, recv, device):
        return pltpu.make_async_remote_copy(
            src_ref=buf.at[k], dst_ref=buf.at[k], send_sem=send, recv_sem=recv,
            device_id=device, device_id_type=MESH,
        )

    def half(buf, k, p, send, recv, device):
        at = buf.at[k, pl.ds(*HALF[p]), :]
        return pltpu.make_async_remote_copy(
            src_ref=at, dst_ref=at, send_sem=send, recv_sem=recv,
            device_id=device, device_id_type=MESH,
        )

    def y_copy(i, way, piece):
        to = ((yup, ydn)[way] * 4 + z, col)
        if piece < 2:
            which, origin = (way, 1 - way)[piece], y
        else:
            which, origin = way, (ydn, yup)[way]
        return half(bbuf, origin * 4 + zorder[i], which, ys.at[i, way, piece], yr.at[i, way, piece], to)

    def y_arrival(i, way, piece):
        if piece < 2:
            which, origin = (way, 1 - way)[piece], (ydn, yup)[way]
        else:
            which, origin = way, (y + 2) % 4
        return half(bbuf, origin * 4 + zorder[i], which, ys.at[i, way, piece], yr.at[i, way, piece], ((yup, ydn)[way] * 4 + z, col))

    def x_piece(i, origin, q, send, recv, way):
        at = abuf.at[col_of(origin, horder[i], core), pl.ds(*XCUT[i][q]), :]
        return pltpu.make_async_remote_copy(
            src_ref=at, dst_ref=at, send_sem=send, recv_sem=recv,
            device_id=(row, col_of((xup, xdn)[way], h, core)), device_id_type=MESH,
        )

    def x_copy(i, way, q):
        return x_piece(i, x, q, xs.at[i, way, q], xr.at[i, way, q], way)

    def x_arrival(i, way, q):
        return x_piece(i, (xdn, xup)[way], q, xs.at[i, way, q], xr.at[i, way, q], way)

    def x_forward(i, q):
        return x_piece(i, (xdn, xup)[q % 2], q, fs.at[i, q], fr.at[i, q], q % 2)

    def x_forwarded(i, q):
        return x_piece(i, (x + 2) % 4, q, fs.at[i, q], fr.at[i, q], q % 2)

    def s_piece(i, d, q, kk):
        at = abuf.at[col_of((x + d) % 4, horder[i], kk), pl.ds(*XCUT[i][q]), :]
        return pltpu.make_async_remote_copy(
            src_ref=at, dst_ref=at, send_sem=ss.at[i, d, q], recv_sem=sr.at[i, d, q],
            device_id=(row, col_of(x, h, 1 - core)), device_id_type=MESH,
        )

    def s_copy(i, d, q):
        return s_piece(i, d, q, core)

    def s_arrival(i, d):
        for q in range(len(XCUT[i])):
            s_piece(i, d, q, 1 - core).wait_recv()

    def cross(q, k=None):
        at = abuf.at[mine_a if k is None else k, pl.ds(*XCUT[1][q]), :]
        return pltpu.make_async_remote_copy(
            src_ref=at, dst_ref=at, send_sem=cs.at[q], recv_sem=cr.at[q],
            device_id=(row, col_of(x, 1 - h, core)), device_id_type=MESH,
        )

    def crossed(q):
        return cross(q, col_of(x, 1 - h, core))

    z_up = whole(bbuf, row, zs.at[0], zr.at[z], (row + 1, col))
    z_down = whole(bbuf, row, zs.at[1], zr.at[z], (row - 1, col))
    has_up, has_down = z < 3, z > 0
    interior = jnp.logical_and(has_up, has_down)
    at_end = jnp.logical_not(interior)

    def z_forward(i):
        to = y * 4 + (3 - z if i == 1 else 3 * hi)
        k = y * 4 + zorder[i]
        return whole(bbuf, k, zs.at[1 + i], zr.at[zorder[i]], (to, col))

    def z_arrival(i):
        k = y * 4 + zorder[i]
        return whole(bbuf, k, zs.at[1 + i], zr.at[zorder[i]], (y * 4 + (z + 1) % 4, col))

    def y_send(i):
        for piece in range(2):
            for way in range(2):
                y_copy(i, way, piece).start()

    def y_turn(i):
        for way in range(2):
            y_arrival(i, way, 0).wait_recv()
            y_copy(i, way, 2).start()

    def x_send(i, q):
        for way in (q % 2, 1 - q % 2):
            x_copy(i, way, q).start()

    def x_cross(q):
        crossed(q).wait_recv()
        x_send(1, q)
        s_copy(1, 0, q).start()

    def x_turn(i, q):
        x_arrival(i, q % 2, q).wait_recv()
        x_forward(i, q).start()
        s_copy(i, (3, 1)[q % 2], q).start()

    def x_near(i, q):
        x_arrival(i, 1 - q % 2, q).wait_recv()
        s_copy(i, (1, 3)[q % 2], q).start()

    def x_far(i, q):
        x_forwarded(i, q).wait_recv()
        s_copy(i, 2, q).start()

    def z_turn(i):
        z_arrival(i).wait_recv()
        pl.when(interior)(lambda: z_forward(i).start())

    def s_rest(i):
        for d in range(4):
            s_arrival(i, d)

    def y_rest(i):
        for way in range(2):
            y_arrival(i, way, 1).wait_recv()
            y_arrival(i, way, 2).wait_recv()

    def expand(buf, k, to, r0, c0):
        ext = buf[k, pl.ds(BODY, 16), :].astype(jnp.float32)
        w = {
            at: jnp.broadcast_to(ext[q : q + 1, :], (16, LANES)).astype(jnp.bfloat16)[None]
            for q, at in enumerate(PAIRS)
        }
        for t in range(4):
            i, j = t // 2, t % 2
            for e in range(2):
                value = None
                for s in range(min(t, 2) + 1):
                    part_of = buf[k, pl.ds(s * SLOT + e * T, T), :]
                    term = part_of.reshape(16, 16, LANES) * w[t, s]
                    value = term if value is None else value + term
                left = j * T + e * LANES
                to[pl.ds(r0 + i * T, T), pl.ds(c0 + left, LANES)] = value.reshape(T, LANES)

    def open_a(i, first, count=4, stride=1):
        def one(n, _):
            k = (first + n // 2 * stride) % 4 * 4 + 2 * horder[i] + n % 2
            expand(abuf, k, ad, 0, pl.multiple_of(k * N, N))
            return 0

        lax.fori_loop(0, 2 * count, one, 0)

    def open_b(i, first, count=4, stride=1):
        def one(n, _):
            k = (first + n * stride) % 4 * 4 + zorder[i]
            expand(bbuf, k, bd, pl.multiple_of(k * N, N), 0)
            return 0

        lax.fori_loop(0, count, one, 0)

    def multiply(k, blocks):
        at = pl.ds(pl.multiple_of(k * N, N), blocks * N)
        acc[...] += jnp.dot(ad[:, at], bd[at, :], preferred_element_type=jnp.float32)

    def products(i, first, count=4, stride=1):
        def one(n, _):
            multiply((first + n * stride) % 4 * 4 + zorder[i], 1)
            return 0

        lax.fori_loop(0, count, one, 0)

    def doubles(hh, first, count=4, stride=1):
        def one(n, _):
            multiply((first + n * stride) % 4 * 4 + 2 * hh, 2)
            return 0

        lax.fori_loop(0, count, one, 0)

    near = hi == h
    far = hi != h

    def late(first, count):
        open_a(1, x + first, count, 2)
        pl.when(far)(lambda: doubles(hi, x + first, count, 2))
        pl.when(near)(lambda: products(2, x + first, count, 2))

    @pl.when(has_up)
    def _():
        z_up.start()

    @pl.when(has_down)
    def _():
        z_down.start()

    y_send(0)
    for q in range(2):
        x_send(0, q)
        s_copy(0, 0, q).start()
    cross(0).start()
    acc[...] = jnp.zeros_like(acc)
    y_turn(0)
    x_turn(0, 0)
    x_turn(0, 1)
    z_turn(1)
    pl.when(interior)(lambda: z_turn(2))
    y_send(1)
    for q in range(2):
        x_near(0, q)
    for q in range(2):
        x_far(0, q)
    s_rest(0)
    y_rest(0)
    y_turn(1)
    cross(1).start()
    open_a(0, x)
    open_b(0, y)
    pl.when(interior)(lambda: z_turn(3))
    pl.when(at_end)(lambda: z_arrival(2).wait_recv())
    y_send(2)
    cross(2).start()
    cross(3).start()
    x_cross(0)
    y_rest(1)
    open_b(1, y)
    pl.when(near)(lambda: doubles(h, y))
    x_turn(1, 0)
    x_near(1, 0)
    y_turn(2)
    pl.when(interior)(lambda: y_send(3))
    x_cross(1)
    x_far(1, 0)
    x_turn(1, 1)
    x_near(1, 1)

    @pl.when(at_end)
    def _():
        z_arrival(3).wait_recv()
        y_send(3)

    y_rest(2)

    open_b(2, y)
    open_b(3, y, 1)

    @pl.when(far)
    def _():
        products(2, y)
        products(3, y, 1)

    x_cross(2)
    x_far(1, 1)
    y_turn(3)
    x_cross(3)
    x_turn(1, 2)
    x_turn(1, 3)
    x_near(1, 2)
    x_near(1, 3)
    s_arrival(1, 0)
    late(0, 1)
    x_far(1, 2)
    x_far(1, 3)
    for way in range(2):
        y_arrival(3, way, 1).wait_recv()
    open_b(3, y + 1, 2, 2)
    pl.when(far)(lambda: products(3, y + 1, 2, 2))
    s_arrival(1, 1)
    s_arrival(1, 3)
    late(1, 2)
    for d in (0, 1, 3):
        pl.when(jnp.logical_and(near, (y + d) % 4 != (x + 2) % 4))(lambda d=d: products(3, y + d, 1))
    for way in range(2):
        y_arrival(3, way, 2).wait_recv()
    open_b(3, y + 2, 1)
    pl.when(jnp.logical_or(far, y != x))(lambda: products(3, y + 2, 1))
    s_arrival(1, 2)
    open_a(1, x + 2, 1)
    doubles(1 - h, x + 2, 1)

    sums = jnp.zeros((8, N), jnp.float32)
    pieces = [[None, None], [None, None]]
    for i in range(2):
        keep = [(masks[2 + i, j] == 1).astype(jnp.float32) for j in range(2)]
        for r in range(i * T, (i + 1) * T, 32):
            for j in range(2):
                at = (slice(r, r + 32), slice(j * T, (j + 1) * T))
                p = acc[at]
                v = p * p * keep[j]
                acc[at] = v
                v = v.reshape(4, 8, T).sum(axis=0)
                pieces[i][j] = v if pieces[i][j] is None else pieces[i][j] + v
    sums = jnp.concatenate([pieces[0][j] + pieces[1][j] for j in range(2)], axis=1)
    sums = jnp.sum(sums, axis=0, keepdims=True)
    part[...] = sums
    tot[row] = sums

    def t_copy(d, i):
        to = (y + d) % 4 * 4 + zorder[i]
        return pltpu.make_async_remote_copy(
            src_ref=part, dst_ref=tot.at[row], send_sem=ts, recv_sem=tr,
            device_id=(to, col), device_id_type=MESH,
        )

    t_all = pltpu.make_async_remote_copy(
        src_ref=tot.at[pl.ds(0, 15)], dst_ref=tot.at[pl.ds(0, 15)], send_sem=ts, recv_sem=tr,
        device_id=((row + 1) % 16, col), device_id_type=MESH,
    )

    peers = [(d, i) for d in (2, 1, 3, 0) for i in (3, 2, 1, 0) if d or i]
    peers.sort(key=lambda at: -(min(at[0], 2) % 3 - (at[0] == 3) + at[1]))
    for d, i in peers:
        t_copy(d, i).start()
    out = pltpu.make_async_copy(acc, infl_ref, osem)
    out.start()

    for i in range(4):
        for way in range(2):
            for piece in range(3):
                y_copy(i, way, piece).wait_send()
    for i in range(2):
        for q in range(len(XCUT[i])):
            for way in range(2):
                x_copy(i, way, q).wait_send()
            x_forward(i, q).wait_send()
            for d in range(4):
                s_copy(i, d, q).wait_send()
    for q in range(4):
        cross(q).wait_send()

    @pl.when(has_up)
    def _():
        z_up.wait_send()

    @pl.when(has_down)
    def _():
        z_down.wait_send()

    @pl.when(interior)
    def _():
        for i in range(1, 4):
            z_forward(i).wait_send()

    t_all.wait_recv()
    total = tot[0]
    for d in range(1, 16):
        total = total + tot[d]
    scale_ref[...] = 1.0 / total
    out.wait()

    t_all.wait_send()


def solution(mesh):
    def step(matrix, in_mask, out_mask):
        total_rows = float(N * mesh.shape["row"])
        dma = pltpu.SemaphoreType.DMA
        inflated, scale = pl.pallas_call(
            kernel,
            out_shape=(
                jax.ShapeDtypeStruct((N, N), jnp.float32),
                jax.ShapeDtypeStruct((1, N), jnp.float32),
            ),
            in_specs=[
                pl.BlockSpec(memory_space=pltpu.HBM),
                pl.BlockSpec(memory_space=pltpu.HBM),
            ],
            out_specs=(
                pl.BlockSpec(memory_space=pl.ANY),
                pl.BlockSpec(memory_space=pltpu.VMEM),
            ),
            scratch_shapes=[
                pltpu.VMEM((N, N), jnp.bfloat16),
                pltpu.SMEM((4, 2), jnp.int32),
                pltpu.VMEM((16, ROWS, LANES), jnp.bfloat16),
                pltpu.VMEM((16, ROWS, LANES), jnp.bfloat16),
                pltpu.VMEM((N, 16 * N), jnp.bfloat16),
                pltpu.VMEM((16 * N, N), jnp.bfloat16),
                pltpu.VMEM((N, N), jnp.float32),
                pltpu.VMEM((16, 1, N), jnp.float32),
                pltpu.VMEM((1, N), jnp.float32),
                dma((4, 2, 3)), dma((4, 2, 3)),
                dma((5,)), dma((4,)),
                dma((2, 2, 4)), dma((2, 2, 4)),
                dma((2, 4)), dma((2, 4)),
                dma((4,)), dma((4,)),
                dma((2, 4, 4)), dma((2, 4, 4)),
                dma, dma,
                dma, dma((3,)),
            ],
            compiler_params=pltpu.CompilerParams(
                collective_id=0, has_side_effects=True, vmem_limit_bytes=40 * 1024 * 1024
            ),
            name="gather_square",
        )(matrix, jnp.concatenate([in_mask, out_mask]))
        return (total_rows * inflated) * scale

    placed = (P("row", "col"), P("row", "col"), P("row", "col"))
    return jax.shard_map(
        step, mesh=mesh, in_specs=placed, out_specs=P("row", "col"), check_vma=False
    )
```

```python
import jax
import jax.numpy as jnp
from jax import lax
from jax.experimental import pallas as pl
from jax.experimental.pallas import tpu as pltpu
from jax.sharding import PartitionSpec as P

MESH = pl.DeviceIdType.MESH
T = 256
N = 2 * T
LANES = 128
SLOT = 2 * T
BODY = 3 * SLOT
ROWS = BODY + 16
CUT = 784
HALF = ((0, CUT), (CUT, ROWS - CUT))
XCUT = (HALF, ((0, 480), (480, 448), (928, 384), (1312, 240)))
PAIRS = tuple((t, s) for t in range(4) for s in range(3) if s <= t)


def kernel(
    m_hbm, masks_hbm, infl_ref, scale_ref,
    m_ref, masks, abuf, bbuf, ad, bd, acc, tot, part,
    ys, yr, zs, zr, xs, xr, fs, fr, cs, cr, ss, sr, ts, tr, osem, isem,
):
    row = lax.axis_index("row")
    col = lax.axis_index("col")
    y, z = row // 4, row % 4
    x, h, core = col // 4, (col // 2) % 2, col % 2
    hi = z // 2
    yup, ydn = (y + 1) % 4, (y + 3) % 4
    xup, xdn = (x + 1) % 4, (x + 3) % 4
    zorder = (z, 1 - z + 4 * hi, 2 - hi, 3 - 3 * hi)
    horder = (h, 1 - h)

    def col_of(xx, hh, kk):
        return xx * 4 + hh * 2 + kk

    loads = [
        pltpu.make_async_copy(src, dst, isem.at[n])
        for n, (src, dst) in enumerate(((masks_hbm, masks), (m_hbm, m_ref)))
    ]
    for load in loads:
        load.start()

    barrier = pltpu.get_barrier_semaphore()
    has_up, has_down = z < 3, z > 0

    def greet(r, c):
        pl.semaphore_signal(barrier, inc=1, device_id=(r, c), device_id_type=MESH)

    greet(row, col_of(x, 1 - h, core))
    greet(yup * 4 + z, col)
    greet(ydn * 4 + z, col)
    pl.when(has_up)(lambda: greet(row + 1, col))
    pl.when(has_down)(lambda: greet(row - 1, col))
    greet(row, col_of(xup, h, core))
    greet(row, col_of(xdn, h, core))
    greet(row, col_of(x, h, 1 - core))

    for load in loads:
        load.wait()
    flags = [masks[0, 0], masks[0, 1], masks[1, 0], masks[1, 1]]
    ranks = [0, flags[0], flags[0] + flags[1], flags[0] + flags[1] + flags[2]]
    here = {(t, s): jnp.logical_and(flags[t] == 1, ranks[t] == s) for t, s in PAIRS}
    mine_b = row
    mine_a = col
    for s in range(3):
        for r in range(0, T, 64):
            value = jnp.zeros((64, T), jnp.bfloat16)
            for t in range(s, 4):
                i, j = t // 2, t % 2
                tile = m_ref[i * T + r : i * T + r + 64, j * T : (j + 1) * T]
                value = lax.select(here[t, s], tile, value)
            for e in range(2):
                at = pl.ds(s * SLOT + e * T + r, 64)
                bbuf[mine_b, at, :] = value[:, e * LANES : (e + 1) * LANES]
                abuf[mine_a, at, :] = value[:, e * LANES : (e + 1) * LANES]
    line = lax.broadcasted_iota(jnp.int32, (16, LANES), 0)
    weights = jnp.zeros((16, LANES), jnp.float32)
    for q, (t, s) in enumerate(PAIRS):
        weights = jnp.where(line == q, here[t, s].astype(jnp.float32), weights)
    weights = weights.astype(jnp.bfloat16)
    bbuf[mine_b, pl.ds(BODY, 16), :] = weights
    abuf[mine_a, pl.ds(BODY, 16), :] = weights

    pl.semaphore_wait(barrier, 6 + has_up.astype(jnp.int32) + has_down.astype(jnp.int32))

    def whole(buf, k, send, recv, device):
        return pltpu.make_async_remote_copy(
            src_ref=buf.at[k], dst_ref=buf.at[k], send_sem=send, recv_sem=recv,
            device_id=device, device_id_type=MESH,
        )

    def half(buf, k, p, send, recv, device):
        at = buf.at[k, pl.ds(*HALF[p]), :]
        return pltpu.make_async_remote_copy(
            src_ref=at, dst_ref=at, send_sem=send, recv_sem=recv,
            device_id=device, device_id_type=MESH,
        )

    def y_copy(i, way, piece):
        to = ((yup, ydn)[way] * 4 + z, col)
        if piece < 2:
            which, origin = (way, 1 - way)[piece], y
        else:
            which, origin = way, (ydn, yup)[way]
        return half(bbuf, origin * 4 + zorder[i], which, ys.at[i, way, piece], yr.at[i, way, piece], to)

    def y_arrival(i, way, piece):
        if piece < 2:
            which, origin = (way, 1 - way)[piece], (ydn, yup)[way]
        else:
            which, origin = way, (y + 2) % 4
        return half(bbuf, origin * 4 + zorder[i], which, ys.at[i, way, piece], yr.at[i, way, piece], ((yup, ydn)[way] * 4 + z, col))

    def x_piece(i, origin, q, send, recv, way):
        at = abuf.at[col_of(origin, horder[i], core), pl.ds(*XCUT[i][q]), :]
        return pltpu.make_async_remote_copy(
            src_ref=at, dst_ref=at, send_sem=send, recv_sem=recv,
            device_id=(row, col_of((xup, xdn)[way], h, core)), device_id_type=MESH,
        )

    def x_copy(i, way, q):
        return x_piece(i, x, q, xs.at[i, way, q], xr.at[i, way, q], way)

    def x_arrival(i, way, q):
        return x_piece(i, (xdn, xup)[way], q, xs.at[i, way, q], xr.at[i, way, q], way)

    def x_forward(i, q):
        return x_piece(i, (xdn, xup)[q % 2], q, fs.at[i, q], fr.at[i, q], q % 2)

    def x_forwarded(i, q):
        return x_piece(i, (x + 2) % 4, q, fs.at[i, q], fr.at[i, q], q % 2)

    def s_piece(i, d, q, kk):
        at = abuf.at[col_of((x + d) % 4, horder[i], kk), pl.ds(*XCUT[i][q]), :]
        return pltpu.make_async_remote_copy(
            src_ref=at, dst_ref=at, send_sem=ss.at[i, d, q], recv_sem=sr.at[i, d, q],
            device_id=(row, col_of(x, h, 1 - core)), device_id_type=MESH,
        )

    def s_copy(i, d, q):
        return s_piece(i, d, q, core)

    def s_arrival(i, d):
        for q in range(len(XCUT[i])):
            s_piece(i, d, q, 1 - core).wait_recv()

    def cross(q, k=None):
        at = abuf.at[mine_a if k is None else k, pl.ds(*XCUT[1][q]), :]
        return pltpu.make_async_remote_copy(
            src_ref=at, dst_ref=at, send_sem=cs.at[q], recv_sem=cr.at[q],
            device_id=(row, col_of(x, 1 - h, core)), device_id_type=MESH,
        )

    def crossed(q):
        return cross(q, col_of(x, 1 - h, core))

    z_up = whole(bbuf, row, zs.at[0], zr.at[z], (row + 1, col))
    z_down = whole(bbuf, row, zs.at[1], zr.at[z], (row - 1, col))
    interior = jnp.logical_and(has_up, has_down)
    at_end = jnp.logical_not(interior)

    def z_forward(i):
        to = y * 4 + (3 - z if i == 1 else 3 * hi)
        k = y * 4 + zorder[i]
        return whole(bbuf, k, zs.at[1 + i], zr.at[zorder[i]], (to, col))

    def z_arrival(i):
        k = y * 4 + zorder[i]
        return whole(bbuf, k, zs.at[1 + i], zr.at[zorder[i]], (y * 4 + (z + 1) % 4, col))

    def y_send(i):
        for piece in range(2):
            for way in range(2):
                y_copy(i, way, piece).start()

    def y_turn(i):
        for way in range(2):
            y_arrival(i, way, 0).wait_recv()
            y_copy(i, way, 2).start()

    def x_send(i, q):
        for way in (q % 2, 1 - q % 2):
            x_copy(i, way, q).start()

    def x_cross(q):
        crossed(q).wait_recv()
        x_send(1, q)
        s_copy(1, 0, q).start()

    def x_turn(i, q):
        x_arrival(i, q % 2, q).wait_recv()
        x_forward(i, q).start()
        s_copy(i, (3, 1)[q % 2], q).start()

    def x_near(i, q):
        x_arrival(i, 1 - q % 2, q).wait_recv()
        s_copy(i, (1, 3)[q % 2], q).start()

    def x_far(i, q):
        x_forwarded(i, q).wait_recv()
        s_copy(i, 2, q).start()

    def z_turn(i):
        z_arrival(i).wait_recv()
        pl.when(interior)(lambda: z_forward(i).start())

    def s_rest(i):
        for d in range(4):
            s_arrival(i, d)

    def y_rest(i):
        for way in range(2):
            y_arrival(i, way, 1).wait_recv()
            y_arrival(i, way, 2).wait_recv()

    def expand(buf, k, to, r0, c0):
        ext = buf[k, pl.ds(BODY, 16), :].astype(jnp.float32)
        w = {
            at: jnp.broadcast_to(ext[q : q + 1, :], (16, LANES)).astype(jnp.bfloat16)[None]
            for q, at in enumerate(PAIRS)
        }
        for t in range(4):
            i, j = t // 2, t % 2
            for e in range(2):
                value = None
                for s in range(min(t, 2) + 1):
                    part_of = buf[k, pl.ds(s * SLOT + e * T, T), :]
                    term = part_of.reshape(16, 16, LANES) * w[t, s]
                    value = term if value is None else value + term
                left = j * T + e * LANES
                to[pl.ds(r0 + i * T, T), pl.ds(c0 + left, LANES)] = value.reshape(T, LANES)

    def open_a(i, first, count=4, stride=1):
        def one(n, _):
            k = (first + n // 2 * stride) % 4 * 4 + 2 * horder[i] + n % 2
            expand(abuf, k, ad, 0, pl.multiple_of(k * N, N))
            return 0

        lax.fori_loop(0, 2 * count, one, 0)

    def open_b(i, first, count=4, stride=1):
        def one(n, _):
            k = (first + n * stride) % 4 * 4 + zorder[i]
            expand(bbuf, k, bd, pl.multiple_of(k * N, N), 0)
            return 0

        lax.fori_loop(0, count, one, 0)

    def multiply(k, blocks):
        at = pl.ds(pl.multiple_of(k * N, N), blocks * N)
        acc[...] += jnp.dot(ad[:, at], bd[at, :], preferred_element_type=jnp.float32)

    def products(i, first, count=4, stride=1):
        def one(n, _):
            multiply((first + n * stride) % 4 * 4 + zorder[i], 1)
            return 0

        lax.fori_loop(0, count, one, 0)

    def doubles(hh, first, count=4, stride=1):
        def one(n, _):
            multiply((first + n * stride) % 4 * 4 + 2 * hh, 2)
            return 0

        lax.fori_loop(0, count, one, 0)

    near = hi == h
    far = hi != h

    def late(first, count):
        open_a(1, x + first, count, 2)
        pl.when(far)(lambda: doubles(hi, x + first, count, 2))
        pl.when(near)(lambda: products(2, x + first, count, 2))

    @pl.when(has_up)
    def _():
        z_up.start()

    @pl.when(has_down)
    def _():
        z_down.start()

    y_send(0)
    for q in range(2):
        x_send(0, q)
        s_copy(0, 0, q).start()
    cross(0).start()
    acc[...] = jnp.zeros_like(acc)
    y_turn(0)
    x_turn(0, 0)
    x_turn(0, 1)
    z_turn(1)
    pl.when(interior)(lambda: z_turn(2))
    y_send(1)
    for q in range(2):
        x_near(0, q)
    for q in range(2):
        x_far(0, q)
    s_rest(0)
    y_rest(0)
    y_turn(1)
    cross(1).start()
    open_a(0, x)
    open_b(0, y)
    pl.when(interior)(lambda: z_turn(3))
    pl.when(at_end)(lambda: z_arrival(2).wait_recv())
    y_send(2)
    cross(2).start()
    x_cross(0)
    y_rest(1)
    open_b(1, y)
    pl.when(near)(lambda: doubles(h, y))
    x_turn(1, 0)
    x_near(1, 0)
    y_turn(2)
    cross(3).start()
    pl.when(interior)(lambda: y_send(3))
    x_cross(1)
    x_far(1, 0)
    x_turn(1, 1)
    x_near(1, 1)

    @pl.when(at_end)
    def _():
        z_arrival(3).wait_recv()
        y_send(3)

    y_rest(2)

    open_b(2, y)
    open_b(3, y, 1)

    @pl.when(far)
    def _():
        products(2, y)
        products(3, y, 1)

    x_cross(2)
    x_far(1, 1)
    y_turn(3)
    x_cross(3)
    x_turn(1, 2)
    x_turn(1, 3)
    x_near(1, 2)
    x_near(1, 3)
    s_arrival(1, 0)
    late(0, 1)
    x_far(1, 2)
    x_far(1, 3)
    for way in range(2):
        y_arrival(3, way, 1).wait_recv()
    open_b(3, y + 1, 2, 2)
    pl.when(far)(lambda: products(3, y + 1, 2, 2))
    s_arrival(1, 1)
    s_arrival(1, 3)
    late(1, 2)
    for d in (0, 1, 3):
        pl.when(jnp.logical_and(near, (y + d) % 4 != (x + 2) % 4))(lambda d=d: products(3, y + d, 1))
    for way in range(2):
        y_arrival(3, way, 2).wait_recv()
    open_b(3, y + 2, 1)
    pl.when(jnp.logical_or(far, y != x))(lambda: products(3, y + 2, 1))
    s_arrival(1, 2)
    open_a(1, x + 2, 1)
    doubles(1 - h, x + 2, 1)

    sums = jnp.zeros((8, N), jnp.float32)
    pieces = [[None, None], [None, None]]
    for i in range(2):
        keep = [(masks[2 + i, j] == 1).astype(jnp.float32) for j in range(2)]
        for r in range(i * T, (i + 1) * T, 32):
            for j in range(2):
                at = (slice(r, r + 32), slice(j * T, (j + 1) * T))
                p = acc[at]
                v = p * p * keep[j]
                acc[at] = v
                v = v.reshape(4, 8, T).sum(axis=0)
                pieces[i][j] = v if pieces[i][j] is None else pieces[i][j] + v
    sums = jnp.concatenate([pieces[0][j] + pieces[1][j] for j in range(2)], axis=1)
    sums = jnp.sum(sums, axis=0, keepdims=True)
    part[...] = sums
    tot[row] = sums

    def t_copy(d, i):
        to = (y + d) % 4 * 4 + zorder[i]
        return pltpu.make_async_remote_copy(
            src_ref=part, dst_ref=tot.at[row], send_sem=ts, recv_sem=tr,
            device_id=(to, col), device_id_type=MESH,
        )

    t_all = pltpu.make_async_remote_copy(
        src_ref=tot.at[pl.ds(0, 15)], dst_ref=tot.at[pl.ds(0, 15)], send_sem=ts, recv_sem=tr,
        device_id=((row + 1) % 16, col), device_id_type=MESH,
    )

    peers = [(d, i) for d in (2, 1, 3, 0) for i in (3, 2, 1, 0) if d or i]
    peers.sort(key=lambda at: -(min(at[0], 2) % 3 - (at[0] == 3) + at[1]))
    for d, i in peers:
        t_copy(d, i).start()
    out = pltpu.make_async_copy(acc, infl_ref, osem)
    out.start()

    for i in range(4):
        for way in range(2):
            for piece in range(3):
                y_copy(i, way, piece).wait_send()
    for i in range(2):
        for q in range(len(XCUT[i])):
            for way in range(2):
                x_copy(i, way, q).wait_send()
            x_forward(i, q).wait_send()
            for d in range(4):
                s_copy(i, d, q).wait_send()
    for q in range(4):
        cross(q).wait_send()

    @pl.when(has_up)
    def _():
        z_up.wait_send()

    @pl.when(has_down)
    def _():
        z_down.wait_send()

    @pl.when(interior)
    def _():
        for i in range(1, 4):
            z_forward(i).wait_send()

    t_all.wait_recv()
    total = tot[0]
    for d in range(1, 16):
        total = total + tot[d]
    scale_ref[...] = 1.0 / total
    out.wait()

    t_all.wait_send()


def solution(mesh):
    def step(matrix, in_mask, out_mask):
        total_rows = float(N * mesh.shape["row"])
        dma = pltpu.SemaphoreType.DMA
        inflated, scale = pl.pallas_call(
            kernel,
            out_shape=(
                jax.ShapeDtypeStruct((N, N), jnp.float32),
                jax.ShapeDtypeStruct((1, N), jnp.float32),
            ),
            in_specs=[
                pl.BlockSpec(memory_space=pltpu.HBM),
                pl.BlockSpec(memory_space=pltpu.HBM),
            ],
            out_specs=(
                pl.BlockSpec(memory_space=pl.ANY),
                pl.BlockSpec(memory_space=pltpu.VMEM),
            ),
            scratch_shapes=[
                pltpu.VMEM((N, N), jnp.bfloat16),
                pltpu.SMEM((4, 2), jnp.int32),
                pltpu.VMEM((16, ROWS, LANES), jnp.bfloat16),
                pltpu.VMEM((16, ROWS, LANES), jnp.bfloat16),
                pltpu.VMEM((N, 16 * N), jnp.bfloat16),
                pltpu.VMEM((16 * N, N), jnp.bfloat16),
                pltpu.VMEM((N, N), jnp.float32),
                pltpu.VMEM((16, 1, N), jnp.float32),
                pltpu.VMEM((1, N), jnp.float32),
                dma((4, 2, 3)), dma((4, 2, 3)),
                dma((5,)), dma((4,)),
                dma((2, 2, 4)), dma((2, 2, 4)),
                dma((2, 4)), dma((2, 4)),
                dma((4,)), dma((4,)),
                dma((2, 4, 4)), dma((2, 4, 4)),
                dma, dma,
                dma, dma((3,)),
            ],
            compiler_params=pltpu.CompilerParams(
                collective_id=0, has_side_effects=True, vmem_limit_bytes=40 * 1024 * 1024
            ),
            name="gather_square",
        )(matrix, jnp.concatenate([in_mask, out_mask]))
        return (total_rows * inflated) * scale

    placed = (P("row", "col"), P("row", "col"), P("row", "col"))
    return jax.shard_map(
        step, mesh=mesh, in_specs=placed, out_specs=P("row", "col"), check_vma=False
    )
```

```python
import jax
import jax.numpy as jnp
from jax import lax
from jax.experimental import pallas as pl
from jax.experimental.pallas import tpu as pltpu
from jax.sharding import PartitionSpec as P

MESH = pl.DeviceIdType.MESH
T = 256
N = 2 * T
LANES = 128
SLOT = 2 * T
BODY = 3 * SLOT
ROWS = BODY + 16
CUT = 784
HALF = ((0, CUT), (CUT, ROWS - CUT))
XCUT = (HALF, ((0, 480), (480, 448), (928, 384), (1312, 240)))
PAIRS = tuple((t, s) for t in range(4) for s in range(3) if s <= t)


def kernel(
    m_hbm, masks_hbm, acc, scale_ref,
    m_ref, masks, abuf, bbuf, ad, bd, tot, part,
    ys, yr, zs, zr, xs, xr, fs, fr, cs, cr, ss, sr, ts, tr, isem,
):
    row = lax.axis_index("row")
    col = lax.axis_index("col")
    y, z = row // 4, row % 4
    x, h, core = col // 4, (col // 2) % 2, col % 2
    hi = z // 2
    yup, ydn = (y + 1) % 4, (y + 3) % 4
    xup, xdn = (x + 1) % 4, (x + 3) % 4
    zorder = (z, 1 - z + 4 * hi, 2 - hi, 3 - 3 * hi)
    horder = (h, 1 - h)

    def col_of(xx, hh, kk):
        return xx * 4 + hh * 2 + kk

    loads = [
        pltpu.make_async_copy(src, dst, isem.at[n])
        for n, (src, dst) in enumerate(((masks_hbm, masks), (m_hbm, m_ref)))
    ]
    for load in loads:
        load.start()

    barrier = pltpu.get_barrier_semaphore()
    has_up, has_down = z < 3, z > 0

    def greet(r, c):
        pl.semaphore_signal(barrier, inc=1, device_id=(r, c), device_id_type=MESH)

    greet(row, col_of(x, 1 - h, core))
    greet(yup * 4 + z, col)
    greet(ydn * 4 + z, col)
    pl.when(has_up)(lambda: greet(row + 1, col))
    pl.when(has_down)(lambda: greet(row - 1, col))
    greet(row, col_of(xup, h, core))
    greet(row, col_of(xdn, h, core))
    greet(row, col_of(x, h, 1 - core))

    for load in loads:
        load.wait()
    flags = [masks[0, 0], masks[0, 1], masks[1, 0], masks[1, 1]]
    ranks = [0, flags[0], flags[0] + flags[1], flags[0] + flags[1] + flags[2]]
    here = {(t, s): jnp.logical_and(flags[t] == 1, ranks[t] == s) for t, s in PAIRS}
    mine_b = row
    mine_a = col
    for s in range(3):
        for r in range(0, T, 64):
            value = jnp.zeros((64, T), jnp.bfloat16)
            for t in range(s, 4):
                i, j = t // 2, t % 2
                tile = m_ref[i * T + r : i * T + r + 64, j * T : (j + 1) * T]
                value = lax.select(here[t, s], tile, value)
            for e in range(2):
                at = pl.ds(s * SLOT + e * T + r, 64)
                bbuf[mine_b, at, :] = value[:, e * LANES : (e + 1) * LANES]
                abuf[mine_a, at, :] = value[:, e * LANES : (e + 1) * LANES]
    line = lax.broadcasted_iota(jnp.int32, (16, LANES), 0)
    weights = jnp.zeros((16, LANES), jnp.float32)
    for q, (t, s) in enumerate(PAIRS):
        weights = jnp.where(line == q, here[t, s].astype(jnp.float32), weights)
    weights = weights.astype(jnp.bfloat16)
    bbuf[mine_b, pl.ds(BODY, 16), :] = weights
    abuf[mine_a, pl.ds(BODY, 16), :] = weights

    pl.semaphore_wait(barrier, 6 + has_up.astype(jnp.int32) + has_down.astype(jnp.int32))

    def whole(buf, k, send, recv, device):
        return pltpu.make_async_remote_copy(
            src_ref=buf.at[k], dst_ref=buf.at[k], send_sem=send, recv_sem=recv,
            device_id=device, device_id_type=MESH,
        )

    def half(buf, k, p, send, recv, device):
        at = buf.at[k, pl.ds(*HALF[p]), :]
        return pltpu.make_async_remote_copy(
            src_ref=at, dst_ref=at, send_sem=send, recv_sem=recv,
            device_id=device, device_id_type=MESH,
        )

    def y_copy(i, way, piece):
        to = ((yup, ydn)[way] * 4 + z, col)
        if piece < 2:
            which, origin = (way, 1 - way)[piece], y
        else:
            which, origin = way, (ydn, yup)[way]
        return half(bbuf, origin * 4 + zorder[i], which, ys.at[i, way, piece], yr.at[i, way, piece], to)

    def y_arrival(i, way, piece):
        if piece < 2:
            which, origin = (way, 1 - way)[piece], (ydn, yup)[way]
        else:
            which, origin = way, (y + 2) % 4
        return half(bbuf, origin * 4 + zorder[i], which, ys.at[i, way, piece], yr.at[i, way, piece], ((yup, ydn)[way] * 4 + z, col))

    def x_piece(i, origin, q, send, recv, way):
        at = abuf.at[col_of(origin, horder[i], core), pl.ds(*XCUT[i][q]), :]
        return pltpu.make_async_remote_copy(
            src_ref=at, dst_ref=at, send_sem=send, recv_sem=recv,
            device_id=(row, col_of((xup, xdn)[way], h, core)), device_id_type=MESH,
        )

    def x_copy(i, way, q):
        return x_piece(i, x, q, xs.at[i, way, q], xr.at[i, way, q], way)

    def x_arrival(i, way, q):
        return x_piece(i, (xdn, xup)[way], q, xs.at[i, way, q], xr.at[i, way, q], way)

    def x_forward(i, q):
        return x_piece(i, (xdn, xup)[q % 2], q, fs.at[i, q], fr.at[i, q], q % 2)

    def x_forwarded(i, q):
        return x_piece(i, (x + 2) % 4, q, fs.at[i, q], fr.at[i, q], q % 2)

    def s_piece(i, d, q, kk):
        at = abuf.at[col_of((x + d) % 4, horder[i], kk), pl.ds(*XCUT[i][q]), :]
        return pltpu.make_async_remote_copy(
            src_ref=at, dst_ref=at, send_sem=ss.at[i, d, q], recv_sem=sr.at[i, d, q],
            device_id=(row, col_of(x, h, 1 - core)), device_id_type=MESH,
        )

    def s_copy(i, d, q):
        return s_piece(i, d, q, core)

    def s_arrival(i, d):
        for q in range(len(XCUT[i])):
            s_piece(i, d, q, 1 - core).wait_recv()

    def cross(q, k=None):
        at = abuf.at[mine_a if k is None else k, pl.ds(*XCUT[1][q]), :]
        return pltpu.make_async_remote_copy(
            src_ref=at, dst_ref=at, send_sem=cs.at[q], recv_sem=cr.at[q],
            device_id=(row, col_of(x, 1 - h, core)), device_id_type=MESH,
        )

    def crossed(q):
        return cross(q, col_of(x, 1 - h, core))

    z_up = whole(bbuf, row, zs.at[0], zr.at[z], (row + 1, col))
    z_down = whole(bbuf, row, zs.at[1], zr.at[z], (row - 1, col))
    interior = jnp.logical_and(has_up, has_down)
    at_end = jnp.logical_not(interior)

    def z_forward(i):
        to = y * 4 + (3 - z if i == 1 else 3 * hi)
        k = y * 4 + zorder[i]
        return whole(bbuf, k, zs.at[1 + i], zr.at[zorder[i]], (to, col))

    def z_arrival(i):
        k = y * 4 + zorder[i]
        return whole(bbuf, k, zs.at[1 + i], zr.at[zorder[i]], (y * 4 + (z + 1) % 4, col))

    def y_send(i):
        for piece in range(2):
            for way in range(2):
                y_copy(i, way, piece).start()

    def y_turn(i):
        for way in range(2):
            y_arrival(i, way, 0).wait_recv()
            y_copy(i, way, 2).start()

    def x_send(i, q):
        for way in (q % 2, 1 - q % 2):
            x_copy(i, way, q).start()

    def x_cross(q):
        crossed(q).wait_recv()
        x_send(1, q)
        s_copy(1, 0, q).start()

    def x_turn(i, q):
        x_arrival(i, q % 2, q).wait_recv()
        x_forward(i, q).start()
        s_copy(i, (3, 1)[q % 2], q).start()

    def x_near(i, q):
        x_arrival(i, 1 - q % 2, q).wait_recv()
        s_copy(i, (1, 3)[q % 2], q).start()

    def x_far(i, q):
        x_forwarded(i, q).wait_recv()
        s_copy(i, 2, q).start()

    def z_turn(i):
        z_arrival(i).wait_recv()
        pl.when(interior)(lambda: z_forward(i).start())

    def s_rest(i):
        for d in range(4):
            s_arrival(i, d)

    def y_rest(i):
        for way in range(2):
            y_arrival(i, way, 1).wait_recv()
            y_arrival(i, way, 2).wait_recv()

    def expand(buf, k, to, r0, c0):
        ext = buf[k, pl.ds(BODY, 16), :].astype(jnp.float32)
        w = {
            at: jnp.broadcast_to(ext[q : q + 1, :], (16, LANES)).astype(jnp.bfloat16)[None]
            for q, at in enumerate(PAIRS)
        }
        for t in range(4):
            i, j = t // 2, t % 2
            for e in range(2):
                value = None
                for s in range(min(t, 2) + 1):
                    part_of = buf[k, pl.ds(s * SLOT + e * T, T), :]
                    term = part_of.reshape(16, 16, LANES) * w[t, s]
                    value = term if value is None else value + term
                left = j * T + e * LANES
                to[pl.ds(r0 + i * T, T), pl.ds(c0 + left, LANES)] = value.reshape(T, LANES)

    def open_a(i, first, count=4, stride=1):
        def one(n, _):
            k = (first + n // 2 * stride) % 4 * 4 + 2 * horder[i] + n % 2
            expand(abuf, k, ad, 0, pl.multiple_of(k * N, N))
            return 0

        lax.fori_loop(0, 2 * count, one, 0)

    def open_b(i, first, count=4, stride=1):
        def one(n, _):
            k = (first + n * stride) % 4 * 4 + zorder[i]
            expand(bbuf, k, bd, pl.multiple_of(k * N, N), 0)
            return 0

        lax.fori_loop(0, count, one, 0)

    def multiply(k, blocks):
        at = pl.ds(pl.multiple_of(k * N, N), blocks * N)
        acc[...] += jnp.dot(ad[:, at], bd[at, :], preferred_element_type=jnp.float32)

    def products(i, first, count=4, stride=1):
        def one(n, _):
            multiply((first + n * stride) % 4 * 4 + zorder[i], 1)
            return 0

        lax.fori_loop(0, count, one, 0)

    def doubles(hh, first, count=4, stride=1):
        def one(n, _):
            multiply((first + n * stride) % 4 * 4 + 2 * hh, 2)
            return 0

        lax.fori_loop(0, count, one, 0)

    near = hi == h
    far = hi != h

    def late(first, count):
        open_a(1, x + first, count, 2)
        pl.when(far)(lambda: doubles(hi, x + first, count, 2))
        pl.when(near)(lambda: products(2, x + first, count, 2))

    @pl.when(has_up)
    def _():
        z_up.start()

    @pl.when(has_down)
    def _():
        z_down.start()

    y_send(0)
    for q in range(2):
        x_send(0, q)
        s_copy(0, 0, q).start()
    cross(0).start()
    acc[...] = jnp.zeros_like(acc)
    y_turn(0)
    x_turn(0, 0)
    x_turn(0, 1)
    z_turn(1)
    pl.when(interior)(lambda: z_turn(2))
    y_send(1)
    for q in range(2):
        x_near(0, q)
    for q in range(2):
        x_far(0, q)
    s_rest(0)
    y_rest(0)
    y_turn(1)
    cross(1).start()
    open_a(0, x)
    open_b(0, y)
    pl.when(interior)(lambda: z_turn(3))
    pl.when(at_end)(lambda: z_arrival(2).wait_recv())
    y_send(2)
    cross(2).start()
    x_cross(0)
    y_rest(1)
    open_b(1, y)
    pl.when(near)(lambda: doubles(h, y))
    x_turn(1, 0)
    x_near(1, 0)
    y_turn(2)
    cross(3).start()
    pl.when(interior)(lambda: y_send(3))
    x_cross(1)
    x_far(1, 0)
    x_turn(1, 1)
    x_near(1, 1)

    @pl.when(at_end)
    def _():
        z_arrival(3).wait_recv()
        y_send(3)

    y_rest(2)

    open_b(2, y)
    open_b(3, y, 1)

    @pl.when(far)
    def _():
        products(2, y)
        products(3, y, 1)

    x_cross(2)
    x_far(1, 1)
    y_turn(3)
    x_cross(3)
    x_turn(1, 2)
    x_turn(1, 3)
    x_near(1, 2)
    x_near(1, 3)
    s_arrival(1, 0)
    late(0, 1)
    x_far(1, 2)
    x_far(1, 3)
    for way in range(2):
        y_arrival(3, way, 1).wait_recv()
    open_b(3, y + 1, 2, 2)
    pl.when(far)(lambda: products(3, y + 1, 2, 2))
    s_arrival(1, 1)
    s_arrival(1, 3)
    late(1, 2)
    for d in (0, 1, 3):
        pl.when(jnp.logical_and(near, (y + d) % 4 != (x + 2) % 4))(lambda d=d: products(3, y + d, 1))
    for way in range(2):
        y_arrival(3, way, 2).wait_recv()
    open_b(3, y + 2, 1)
    pl.when(jnp.logical_or(far, y != x))(lambda: products(3, y + 2, 1))
    s_arrival(1, 2)
    open_a(1, x + 2, 1)
    doubles(1 - h, x + 2, 1)

    sums = jnp.zeros((8, N), jnp.float32)
    pieces = [[None, None], [None, None]]
    for i in range(2):
        keep = [(masks[2 + i, j] == 1).astype(jnp.float32) for j in range(2)]
        for r in range(i * T, (i + 1) * T, 32):
            for j in range(2):
                at = (slice(r, r + 32), slice(j * T, (j + 1) * T))
                p = acc[at]
                v = p * p * keep[j]
                acc[at] = v
                v = v.reshape(4, 8, T).sum(axis=0)
                pieces[i][j] = v if pieces[i][j] is None else pieces[i][j] + v
    sums = jnp.concatenate([pieces[0][j] + pieces[1][j] for j in range(2)], axis=1)
    sums = jnp.sum(sums, axis=0, keepdims=True)
    part[...] = sums
    tot[row] = sums

    def t_copy(d, i):
        to = (y + d) % 4 * 4 + zorder[i]
        return pltpu.make_async_remote_copy(
            src_ref=part, dst_ref=tot.at[row], send_sem=ts, recv_sem=tr,
            device_id=(to, col), device_id_type=MESH,
        )

    t_all = pltpu.make_async_remote_copy(
        src_ref=tot.at[pl.ds(0, 15)], dst_ref=tot.at[pl.ds(0, 15)], send_sem=ts, recv_sem=tr,
        device_id=((row + 1) % 16, col), device_id_type=MESH,
    )

    peers = [(d, i) for d in (2, 1, 3, 0) for i in (3, 2, 1, 0) if d or i]
    peers.sort(key=lambda at: -(min(at[0], 2) % 3 - (at[0] == 3) + at[1]))
    for d, i in peers:
        t_copy(d, i).start()

    for i in range(4):
        for way in range(2):
            for piece in range(3):
                y_copy(i, way, piece).wait_send()
    for i in range(2):
        for q in range(len(XCUT[i])):
            for way in range(2):
                x_copy(i, way, q).wait_send()
            x_forward(i, q).wait_send()
            for d in range(4):
                s_copy(i, d, q).wait_send()
    for q in range(4):
        cross(q).wait_send()

    @pl.when(has_up)
    def _():
        z_up.wait_send()

    @pl.when(has_down)
    def _():
        z_down.wait_send()

    @pl.when(interior)
    def _():
        for i in range(1, 4):
            z_forward(i).wait_send()

    t_all.wait_recv()
    total = jnp.sum(tot[...], axis=0)
    scale_ref[...] = 1.0 / total

    t_all.wait_send()


def solution(mesh):
    def step(matrix, in_mask, out_mask):
        total_rows = float(N * mesh.shape["row"])
        dma = pltpu.SemaphoreType.DMA
        inflated, scale = pl.pallas_call(
            kernel,
            out_shape=(
                jax.ShapeDtypeStruct((N, N), jnp.float32),
                jax.ShapeDtypeStruct((1, N), jnp.float32),
            ),
            in_specs=[
                pl.BlockSpec(memory_space=pltpu.HBM),
                pl.BlockSpec(memory_space=pltpu.HBM),
            ],
            out_specs=(
                pl.BlockSpec(memory_space=pltpu.VMEM),
                pl.BlockSpec(memory_space=pltpu.VMEM),
            ),
            scratch_shapes=[
                pltpu.VMEM((N, N), jnp.bfloat16),
                pltpu.SMEM((4, 2), jnp.int32),
                pltpu.VMEM((16, ROWS, LANES), jnp.bfloat16),
                pltpu.VMEM((16, ROWS, LANES), jnp.bfloat16),
                pltpu.VMEM((N, 16 * N), jnp.bfloat16),
                pltpu.VMEM((16 * N, N), jnp.bfloat16),
                pltpu.VMEM((16, 1, N), jnp.float32),
                pltpu.VMEM((1, N), jnp.float32),
                dma((4, 2, 3)), dma((4, 2, 3)),
                dma((5,)), dma((4,)),
                dma((2, 2, 4)), dma((2, 2, 4)),
                dma((2, 4)), dma((2, 4)),
                dma((4,)), dma((4,)),
                dma((2, 4, 4)), dma((2, 4, 4)),
                dma, dma,
                dma((3,)),
            ],
            compiler_params=pltpu.CompilerParams(
                collective_id=0, has_side_effects=True, vmem_limit_bytes=40 * 1024 * 1024
            ),
            name="gather_square",
        )(matrix, jnp.concatenate([in_mask, out_mask]))
        return (total_rows * inflated) * scale

    placed = (P("row", "col"), P("row", "col"), P("row", "col"))
    return jax.shard_map(
        step, mesh=mesh, in_specs=placed, out_specs=P("row", "col"), check_vma=False
    )
```
